32 devices in a mesh: groups: 2 (over y), dp: 4 (over z), query: 4 (over x, core).
Axes of the slice: x: 2, y: 2, z: 4, core: 2. Of those that a mesh axis runs over, the one named last changes fastest.
Arguments:
- queries: float32 [512, 2048], P(('groups', 'query')), parts along dimension 0, may hold values from -6 to 6
- train_grads: float32 [8192, 2048], P(('groups', 'dp', 'query')), parts along dimension 0, as said below
- factor: bfloat16 [4096, 2048], P('groups'), parts along dimension 0, as said below
Outputs:
- scores: float32 [512, 4096], P('groups', ('dp', 'query')), parts along dimension 0
The draws below stay inside these ranges and needn't reach their ends.
There are 2 independent parts, one for each index of `groups`. The reference program is written for one: setup_inputs(seed, part) draws one part's arguments, and reference() takes and returns one part's arrays. A program takes and returns all parts, laid end to end along the dimension named above; each array names one. Nothing has to cross between parts.
Inputs may be any that keep to these rules, and one draw needn't show every extreme that they name: `train_grads`: each row of training gradients is a product of a row scale, a column scale and independent entries. `factor`: lower triangular with a positive diagonal.
All inputs are finite; a program needn't handle non-finite values.
Results may differ from the reference program's by a relative error of at most 0.0003.
Values sent between devices are 32-bit elements; how exact they have to be, the bound alone decides.
No kernel may reach another device: no remote copies, remote signals or barrier semaphores. Data moves between devices by JAX's collectives and lax.ppermute only.
A program may use at most 128 MiB of HBM per device.

```python
import math
import jax
import jax.numpy as jnp
from jax import lax

K = 2048
NTRAIN = 4096
QUERIES = 256


def column_scales(key):
    return jnp.exp(jax.random.uniform(key, (K,), jnp.float32, 0.0, math.log(10.0)))


def draw_train_grads(key, part):
    columns = column_scales(key)
    key = jax.random.fold_in(key, 1)
    first_key, second_key = jax.random.split(key)
    row_scale = jnp.exp(jax.random.uniform(first_key, (NTRAIN, 1), jnp.float32, 0.0, math.log(10.0))) / jnp.sqrt(21.5)
    entries = jax.random.truncated_normal(second_key, -4.0, 4.0, (NTRAIN, K), jnp.float32)
    return row_scale * columns[None, :] * entries


def draw_factor(key, part):
    columns = column_scales(key)
    key = jax.random.fold_in(key, 2)
    first_key, second_key = jax.random.split(key)
    spread = jax.random.uniform(first_key, (K,), jnp.float32, 1.0, 1.4)
    below = jax.random.uniform(second_key, (K, K), jnp.float32, -3.0, 3.0) * K ** (-0.5) * columns[:, None]
    index = jnp.arange(K)
    lower = jnp.where(index[:, None] > index[None, :], below, 0.0)
    lower = lower + jnp.where(index[:, None] == index[None, :], (columns * spread)[:, None], 0.0)
    return lower.astype(jnp.bfloat16)


def block_scale(key, extent, cuts, smallest, top_value):
    def one(dim, parts):
        heights = jax.random.uniform(jax.random.fold_in(jax.random.fold_in(key, 6), dim), (parts,), jnp.float32, smallest / len(cuts), top_value / len(cuts))
        return jnp.repeat(jnp.exp(heights), extent[dim] // parts).reshape((-1,) + (1,) * (len(extent) - dim - 1))

    gain = one(*cuts[0])
    for cut in cuts[1:]:
        gain = gain * one(*cut)
    return gain


def centred(stream_key, extent, deviation, limit, shards=(), kind=jnp.bfloat16):
    array = deviation * jax.random.normal(stream_key, extent, jnp.float32)
    if shards:
        array = array * block_scale(stream_key, extent, shards, -0.22, 0.18)
    return jnp.clip(array, -limit, limit).astype(kind)


def setup_inputs(seed: int = 0, part: int = 0) -> dict:
    streams_of = jax.random.split(jax.random.key(seed), 4)
    part_splits = jax.random.split(jax.random.fold_in(streams_of[3], part), 4)
    return {
        "queries": centred(part_splits[0], (QUERIES, K), 1.0, 6.0, ((0, 4),), jnp.float32),
        "train_grads": draw_train_grads(jax.random.fold_in(jax.random.fold_in(streams_of[3], part), 71), part),
        "factor": draw_factor(jax.random.fold_in(jax.random.fold_in(streams_of[3], part), 71), part),
    }


def precond(lower, values):
    inner = lax.linalg.triangular_solve(lower, values, left_side=False, lower=True, transpose_a=True)
    return lax.linalg.triangular_solve(lower, inner, left_side=False, lower=True, transpose_a=False)

def reference(queries, train_grads, factor):
    gram = lax.dot_general(train_grads.astype(jnp.float32), train_grads.astype(jnp.float32), (((0,), (0,)), ((), ())), precision=lax.Precision.HIGHEST, preferred_element_type=jnp.float32)
    system = gram / NTRAIN + 0.5 * jnp.eye(K, dtype=jnp.float32)
    lower = factor.astype(jnp.float32)
    first = precond(lower, queries)
    defect = queries - jnp.dot(first.astype(jnp.float32), system.astype(jnp.float32), precision=lax.Precision.HIGHEST, preferred_element_type=jnp.float32)
    refined = first + precond(lower, defect)
    scale_factor = 1.0 / jnp.sqrt(jnp.float32(K))
    return jnp.dot(refined.astype(jnp.float32), train_grads.T.astype(jnp.float32), precision=lax.Precision.HIGHEST, preferred_element_type=jnp.float32) * scale_factor
```

```python
import functools

import jax
import jax.numpy as jnp
from jax import lax
from jax.experimental import pallas as pl
from jax.experimental.pallas import tpu as pltpu
from jax.sharding import PartitionSpec as P

BLOCK = 256
HALF = 128
BASE = 16
AXES = ("dp", "query")
F32 = jnp.float32
BF16 = jnp.bfloat16


def split(value):
    high = value.astype(BF16)
    return high, (value - high.astype(F32)).astype(BF16)


def dot_nn(left, right):
    return lax.dot_general(left, right, (((1,), (0,)), ((), ())), preferred_element_type=F32)


def dot_nt(left, right):
    return lax.dot_general(left, right, (((1,), (1,)), ((), ())), preferred_element_type=F32)


def times_exact(left_pair, right, dot):
    rows = left_pair[0].shape[0]
    both = dot(jnp.concatenate(left_pair, axis=0), right)
    return both[:rows] + both[rows:]


def times_pair(left_pair, right_pair, dot):
    return times_exact(left_pair, right_pair[0], dot) + dot(left_pair[0], right_pair[1])


def invert_diagonals(lower, inv_high, inv_low, blocks):
    count = blocks * (BLOCK // HALF)
    row = lax.broadcasted_iota(jnp.int32, (HALF, HALF), 0)
    lane = lax.broadcasted_iota(jnp.int32, (HALF, HALF), 1)
    same = (row // BASE) == (lane // BASE)
    diagonals = [lower[pl.ds(HALF * g, HALF), pl.ds(HALF * g, HALF)].astype(F32) for g in range(count)]
    packed = []
    for diagonal in diagonals:
        kept = jnp.where(same, diagonal, 0.0)
        total = kept[0:BASE]
        for s in range(1, HALF // BASE):
            total = total + kept[s * BASE : (s + 1) * BASE]
        packed.append(total)
    packed = jnp.concatenate(packed, axis=0).astype(BF16)
    shape = (count, BASE, HALF)
    in_row = lax.broadcasted_iota(jnp.int32, shape, 1)
    in_lane = lax.broadcasted_iota(jnp.int32, shape, 2) % BASE
    solved = jnp.where(in_row == in_lane, 1.0, 0.0).astype(F32)
    for k in range(BASE):
        spread = jnp.where(row == (lane // BASE) * BASE + k, 1.0, 0.0).astype(BF16)
        column = dot_nn(packed, spread).reshape(shape)
        pivot_row = solved[:, k : k + 1, :] / column[:, k : k + 1, :]
        below = solved - column * pivot_row
        solved = jnp.where(in_row == k, pivot_row, jnp.where(in_row > k, below, solved))
    inverses = []
    for g in range(count):
        tiled = jnp.concatenate([solved[g]] * (HALF // BASE), axis=0)
        inverses.append(jnp.where(same, tiled, 0.0))
    size = BASE
    while size < HALF:
        part = (row // (2 * size) == lane // (2 * size)) & ((row // size) % 2 == 1) & ((lane // size) % 2 == 0)
        pairs = [split(x) for x in inverses]
        middles = []
        for g in range(count):
            below = jnp.where(part, diagonals[g], 0.0).astype(BF16)
            middles.append(
                dot_nn(jnp.concatenate([below, below], axis=1), jnp.concatenate(pairs[g], axis=0))
            )
        for g in range(count):
            mid_high, mid_low = split(middles[g])
            change = dot_nn(
                jnp.concatenate(pairs[g], axis=1), jnp.concatenate([mid_high, mid_high], axis=0)
            ) + dot_nn(pairs[g][0], mid_low)
            inverses[g] = inverses[g] - change
        size *= 2
    for j in range(blocks):
        upper, under = split(inverses[2 * j]), split(inverses[2 * j + 1])
        below = lower[pl.ds(BLOCK * j + HALF, HALF), pl.ds(BLOCK * j, HALF)]
        middle = dot_nn(jnp.concatenate([below, below], axis=1), jnp.concatenate(upper, axis=0))
        mid_high, mid_low = split(middle)
        corner = dot_nn(
            jnp.concatenate(under, axis=1), jnp.concatenate([mid_high, mid_high], axis=0)
        ) + dot_nn(under[0], mid_low)
        corner = split(-corner)
        zero = jnp.zeros((HALF, HALF), BF16)
        for part, out in ((0, inv_high), (1, inv_low)):
            out[j, 0:HALF, 0:HALF] = upper[part]
            out[j, 0:HALF, HALF:BLOCK] = zero
            out[j, HALF:BLOCK, 0:HALF] = corner[part]
            out[j, HALF:BLOCK, HALF:BLOCK] = under[part]


def solve_kernel(
    factor, train, query, out_high, out_low,
    lower, state, y_high, y_low, inv_high, inv_low, diag_sems, row_sems,
):
    blocks = factor.shape[0] // BLOCK
    rows = train.shape[0]
    extra = query.shape[0]

    def block(j):
        return pl.ds(BLOCK * j, BLOCK)

    diag_copies = [
        pltpu.make_async_copy(factor.at[block(j), block(j)], lower.at[block(j), block(j)], diag_sems.at[j])
        for j in range(blocks)
    ]
    row_copies = [
        pltpu.make_async_copy(
            factor.at[block(j), pl.ds(0, BLOCK * j)], lower.at[block(j), pl.ds(0, BLOCK * j)], row_sems.at[j]
        )
        for j in range(1, blocks)
    ]
    for copy in diag_copies:
        copy.start()
    for copy in row_copies:
        copy.start()
    state[0:rows, :] = train[...]
    state[rows : rows + extra, :] = query[...]
    for copy in diag_copies:
        copy.wait()
    invert_diagonals(lower, inv_high, inv_low, blocks)
    for j in range(blocks):
        value = state[:, block(j)]
        if j == 1:
            row_copies[0].wait()
        if j:
            value = value - times_exact(
                (y_high[:, block(j - 1)], y_low[:, block(j - 1)]), lower[block(j), block(j - 1)], dot_nt
            )
        value = times_pair(split(value), (inv_high[j], inv_low[j]), dot_nt)
        state[:, block(j)] = value
        y_high[:, block(j)], y_low[:, block(j)] = split(value)
        if 1 <= j < blocks - 1:
            row_copies[j].wait()
            done = pl.ds(0, BLOCK * j)
            state[:, block(j + 1)] = state[:, block(j + 1)] - times_exact(
                (y_high[:, done], y_low[:, done]), lower[block(j + 1), done], dot_nt
            )
    for j in reversed(range(blocks)):
        value = state[:, block(j)]
        if j < blocks - 1:
            value = value - times_exact(
                (out_high[:, block(j + 1)], out_low[:, block(j + 1)]), lower[block(j + 1), block(j)], dot_nn
            )
        value = times_pair(split(value), (inv_high[j], inv_low[j]), dot_nn)
        out_high[:, block(j)], out_low[:, block(j)] = split(value)
        if 1 <= j < blocks - 1:
            done = pl.ds(BLOCK * (j + 1), BLOCK * (blocks - 1 - j))
            state[:, block(j - 1)] = state[:, block(j - 1)] - times_exact(
                (out_high[:, done], out_low[:, done]), lower[done, block(j - 1)], dot_nn
            )


def solve(factor, train, query):
    width = factor.shape[0]
    rows = train.shape[0] + query.shape[0]
    blocks = width // BLOCK
    pair = jax.ShapeDtypeStruct((rows, width), BF16)
    return pl.pallas_call(
        solve_kernel,
        out_shape=(pair, pair),
        in_specs=[
            pl.BlockSpec(memory_space=pltpu.HBM),
            pl.BlockSpec(memory_space=pltpu.VMEM),
            pl.BlockSpec(memory_space=pltpu.VMEM),
        ],
        out_specs=(pl.BlockSpec(memory_space=pltpu.VMEM),) * 2,
        scratch_shapes=[
            pltpu.VMEM((width, width), BF16),
            pltpu.VMEM((rows, width), F32),
            pltpu.VMEM((rows, width), BF16),
            pltpu.VMEM((rows, width), BF16),
            pltpu.VMEM((blocks, BLOCK, BLOCK), BF16),
            pltpu.VMEM((blocks, BLOCK, BLOCK), BF16),
            pltpu.SemaphoreType.DMA((blocks,)),
            pltpu.SemaphoreType.DMA((blocks,)),
        ],
        compiler_params=pltpu.CompilerParams(vmem_limit_bytes=40 * 1024 * 1024),
        cost_estimate=pl.CostEstimate(
            flops=12 * rows * width * width, bytes_accessed=16 * 1024 * 1024, transcendentals=0
        ),
        name="solve",
    )(factor, train, query)


def local_kernel(
    scale, extra, where, *refs,
):
    pieces = refs[: -7]
    high, low, train, scores, send, keep, rows_buf = refs[-7:]
    piece_rows = pieces[0].shape[0]
    n_rows = piece_rows * len(pieces)
    for r, piece in enumerate(pieces):
        offset = pl.multiple_of((where[0] ^ r) * piece_rows, piece_rows)
        part_high, part_low = split(piece[...])
        rows_buf[pl.ds(offset, piece_rows), :] = part_high
        rows_buf[pl.ds(offset + n_rows, piece_rows), :] = part_low
    count = train.shape[0]
    weights_high, weights_low = high[0:count, :], low[0:count, :]
    both = dot_nt(rows_buf[...], weights_high)
    found = both[:n_rows] + both[n_rows:] + dot_nt(rows_buf[0:n_rows, :], weights_low)
    scores[...] = found
    pair = split(found * scale)
    n_pieces = 2 * send.shape[0]
    offset = pl.multiple_of(where[2], extra)
    factor = jnp.where(where[3] > 0, 0.5, 0.0).astype(F32)
    for place in range(n_pieces):
        at = place % (n_pieces // 2)
        out, order = (keep, where[1]) if place < n_pieces // 2 else (send, where[4])
        columns = pl.ds(pl.multiple_of((order ^ at) * BLOCK, BLOCK), BLOCK)
        out[at] = times_pair(pair, split(train[:, columns]), dot_nn)
        first = high[pl.ds(count, extra), columns].astype(F32) + low[pl.ds(count, extra), columns].astype(F32)
        out[at, pl.ds(offset, extra), :] = out[at, pl.ds(offset, extra), :] + factor * first


def local(where, pieces, high, low, train, extra, scale):
    n_rows = pieces[0].shape[0] * len(pieces)
    count, width = train.shape
    half = jax.ShapeDtypeStruct((width // BLOCK // 2, n_rows, BLOCK), F32)
    return pl.pallas_call(
        functools.partial(local_kernel, scale, extra),
        out_shape=(jax.ShapeDtypeStruct((n_rows, count), F32), half, half),
        in_specs=[pl.BlockSpec(memory_space=pltpu.SMEM)]
        + [pl.BlockSpec(memory_space=pltpu.VMEM)] * (len(pieces) + 3),
        out_specs=(pl.BlockSpec(memory_space=pltpu.VMEM),) * 3,
        scratch_shapes=[pltpu.VMEM((2 * n_rows, width), BF16)],
        compiler_params=pltpu.CompilerParams(vmem_limit_bytes=40 * 1024 * 1024),
        cost_estimate=pl.CostEstimate(
            flops=12 * n_rows * width * count, bytes_accessed=8 * 1024 * 1024, transcendentals=0
        ),
        name="local",
    )(where, *pieces, high, low, train)


def final_kernel(scale, where, scores, own, other, high, low, out):
    half = own.shape[0]
    count = out.shape[1]
    total = 2.0 * scores[...]
    for place in range(2 * half):
        at = place % half
        source, order = (own, where[1]) if place < half else (other, where[4])
        columns = pl.ds(pl.multiple_of((order ^ at) * BLOCK, BLOCK), BLOCK)
        total = total - times_pair(
            split(source[at]), (high[0:count, columns], low[0:count, columns]), dot_nt
        )
    out[...] = total * scale


def final(where, scores, own, other, high, low, scale):
    n_rows, count = scores.shape
    return pl.pallas_call(
        functools.partial(final_kernel, scale),
        out_shape=jax.ShapeDtypeStruct((n_rows, count), F32),
        in_specs=[pl.BlockSpec(memory_space=pltpu.SMEM)] + [pl.BlockSpec(memory_space=pltpu.VMEM)] * 5,
        out_specs=pl.BlockSpec(memory_space=pltpu.VMEM),
        compiler_params=pltpu.CompilerParams(vmem_limit_bytes=40 * 1024 * 1024),
        name="final",
    )(where, scores, own, other, high, low)


def bits(size):
    assert size & (size - 1) == 0
    return [1 << i for i in range(size.bit_length() - 1)]


def shards(queries, train_grads, factor):
    n_query, n_data = lax.axis_size("query"), lax.axis_size("dp")
    query_pos, data_pos = lax.axis_index("query"), lax.axis_index("dp")
    query_rows, width = queries.shape
    total_train = train_grads.shape[0] * n_data * n_query
    ranks = range(n_query * n_data)

    def swap(value, even, odd=None):
        odd = even if odd is None else odd
        return lax.ppermute(value, AXES, [(r, r ^ (odd if r & 1 else even)) for r in ranks])

    x_bits, z_bits = bits(n_query)[1:], [n_query * b for b in bits(n_data)]
    evens, odds = [], []
    for i in range(max(len(x_bits), len(z_bits))):
        evens += x_bits[i : i + 1] + z_bits[i : i + 1]
        odds += z_bits[i : i + 1] + x_bits[i : i + 1]
    steps = [(1, 1)] + list(zip(evens, odds))

    extra = max(16, query_rows // n_data)
    taken = data_pos * extra < query_rows
    start = jnp.where(taken, data_pos * extra, 0)
    rank = data_pos * n_query + query_pos
    n_pieces = width // BLOCK
    halvings = bits(n_pieces)[::-1]

    def order_of(rank):
        order = jnp.int32(0)
        for weight, (even, odd) in zip(halvings, steps):
            bit = jnp.where(rank & 1, odd, even)
            order = order + jnp.where((rank & bit) != 0, weight, 0)
        return order

    where = jnp.stack(
        [query_pos, order_of(rank), query_pos * query_rows + start, taken.astype(jnp.int32), order_of(rank ^ 1)]
    )

    high, low = solve(factor, train_grads, lax.dynamic_slice_in_dim(queries, start, extra, 0))
    pieces = [queries]
    for bit in x_bits + [1]:
        if bit == 1:
            pieces, high = lax.optimization_barrier((pieces, high))
        moved = swap(jnp.concatenate(pieces, axis=0) if len(pieces) > 1 else pieces[0], bit)
        pieces = pieces + [moved[i * query_rows : (i + 1) * query_rows] for i in range(len(pieces))]
    index = [0]
    for bit in x_bits + [1]:
        index = index + [i ^ bit for i in index]
    pieces = [pieces[index.index(r)] for r in range(n_query)]

    scores, send, keep = local(where, pieces, high, low, train_grads, extra, 1.0 / total_train)

    got = swap(send, *steps[0])
    count = keep.shape[0]
    trail = [steps[0]]
    for step in steps[1:]:
        if count > 1 and len(trail) < len(halvings):
            count //= 2
            send, keep = keep[count:] + got[count:], keep[:count] + got[:count]
            trail.append(step)
            got = swap(send, *step)
        else:
            keep = keep + got
            got = swap(keep, *step)
    own = keep + got
    for step in reversed(trail[1:]):
        own = jnp.concatenate([own, swap(own, *step)], axis=0)
    other = swap(own, *trail[0])
    return final(where, scores, own, other, high, low, width**-0.5)


def solution(mesh):
    in_specs = (P(("groups", "query"), None), P(("groups", "dp", "query"), None), P("groups", None))
    out_specs = P("groups", ("dp", "query"))
    return jax.shard_map(shards, mesh=mesh, in_specs=in_specs, out_specs=out_specs, check_vma=False)
```

```python
import functools

import jax
import jax.numpy as jnp
from jax import lax
from jax.experimental import pallas as pl
from jax.experimental.pallas import tpu as pltpu
from jax.sharding import PartitionSpec as P

BLOCK = 256
HALF = 128
BASE = 16
AXES = ("dp", "query")
F32 = jnp.float32
BF16 = jnp.bfloat16


def split(value):
    high = value.astype(BF16)
    return high, (value - high.astype(F32)).astype(BF16)


def dot_nn(left, right):
    return lax.dot_general(left, right, (((1,), (0,)), ((), ())), preferred_element_type=F32)


def dot_nt(left, right):
    return lax.dot_general(left, right, (((1,), (1,)), ((), ())), preferred_element_type=F32)


def times_exact(left_pair, right, dot):
    rows = left_pair[0].shape[0]
    both = dot(jnp.concatenate(left_pair, axis=0), right)
    return both[:rows] + both[rows:]


def times_pair(left_pair, right_pair, dot):
    return times_exact(left_pair, right_pair[0], dot) + dot(left_pair[0], right_pair[1])


def invert_diagonals(lower, inv_high, inv_low, blocks):
    count = blocks * (BLOCK // HALF)
    row = lax.broadcasted_iota(jnp.int32, (HALF, HALF), 0)
    lane = lax.broadcasted_iota(jnp.int32, (HALF, HALF), 1)
    same = (row // BASE) == (lane // BASE)
    diagonals = [lower[pl.ds(HALF * g, HALF), pl.ds(HALF * g, HALF)].astype(F32) for g in range(count)]
    packed = []
    for diagonal in diagonals:
        kept = jnp.where(same, diagonal, 0.0)
        total = kept[0:BASE]
        for s in range(1, HALF // BASE):
            total = total + kept[s * BASE : (s + 1) * BASE]
        packed.append(total)
    packed = jnp.concatenate(packed, axis=0).astype(BF16)
    shape = (count, BASE, HALF)
    in_row = lax.broadcasted_iota(jnp.int32, shape, 1)
    in_lane = lax.broadcasted_iota(jnp.int32, shape, 2) % BASE
    solved = jnp.where(in_row == in_lane, 1.0, 0.0).astype(F32)
    for k in range(BASE):
        spread = jnp.where(row == (lane // BASE) * BASE + k, 1.0, 0.0).astype(BF16)
        column = dot_nn(packed, spread).reshape(shape)
        pivot_row = solved[:, k : k + 1, :] / column[:, k : k + 1, :]
        below = solved - column * pivot_row
        solved = jnp.where(in_row == k, pivot_row, jnp.where(in_row > k, below, solved))
    inverses = []
    for g in range(count):
        tiled = jnp.concatenate([solved[g]] * (HALF // BASE), axis=0)
        inverses.append(jnp.where(same, tiled, 0.0))
    size = BASE
    while size < HALF:
        part = (row // (2 * size) == lane // (2 * size)) & ((row // size) % 2 == 1) & ((lane // size) % 2 == 0)
        pairs = [split(x) for x in inverses]
        middles = []
        for g in range(count):
            below = jnp.where(part, diagonals[g], 0.0).astype(BF16)
            middles.append(
                dot_nn(jnp.concatenate([below, below], axis=1), jnp.concatenate(pairs[g], axis=0))
            )
        for g in range(count):
            mid_high, mid_low = split(middles[g])
            change = dot_nn(
                jnp.concatenate(pairs[g], axis=1), jnp.concatenate([mid_high, mid_high], axis=0)
            ) + dot_nn(pairs[g][0], mid_low)
            inverses[g] = inverses[g] - change
        size *= 2
    for j in range(blocks):
        upper, under = split(inverses[2 * j]), split(inverses[2 * j + 1])
        below = lower[pl.ds(BLOCK * j + HALF, HALF), pl.ds(BLOCK * j, HALF)]
        middle = dot_nn(jnp.concatenate([below, below], axis=1), jnp.concatenate(upper, axis=0))
        mid_high, mid_low = split(middle)
        corner = dot_nn(
            jnp.concatenate(under, axis=1), jnp.concatenate([mid_high, mid_high], axis=0)
        ) + dot_nn(under[0], mid_low)
        corner = split(-corner)
        zero = jnp.zeros((HALF, HALF), BF16)
        for part, out in ((0, inv_high), (1, inv_low)):
            out[j, 0:HALF, 0:HALF] = upper[part]
            out[j, 0:HALF, HALF:BLOCK] = zero
            out[j, HALF:BLOCK, 0:HALF] = corner[part]
            out[j, HALF:BLOCK, HALF:BLOCK] = under[part]


def solve_kernel(
    where, factor, train, query, out_high, out_low, train_high, train_low,
    lower, state, y_high, y_low, inv_high, inv_low, sems,
):
    blocks = factor.shape[0] // BLOCK
    count = train.shape[0]
    extra = state.shape[0] - count

    def block(j):
        return pl.ds(BLOCK * j, BLOCK)

    def fetch(source, target, at):
        return pltpu.make_async_copy(source, target, sems.at[at])

    diagonal = [
        fetch(factor.at[block(j), block(j)], lower.at[block(j), block(j)], j) for j in range(blocks)
    ]
    start = pl.multiple_of(where[5], extra)
    rest = [
        fetch(train, state.at[pl.ds(0, count), :], blocks),
        fetch(query.at[pl.ds(start, extra), :], state.at[pl.ds(count, extra), :], blocks + 1),
    ]
    for j in range(1, blocks):
        columns = pl.ds(0, BLOCK * j)
        rest.append(fetch(factor.at[block(j), columns], lower.at[block(j), columns], blocks + 1 + j))
    for copy in diagonal + rest:
        copy.start()
    for copy in diagonal:
        copy.wait()
    invert_diagonals(lower, inv_high, inv_low, blocks)
    for copy in rest:
        copy.wait()
    train_high[...], train_low[...] = split(state[0:count, :])

    middle = 16 * -(-(count + extra) // 32)
    groups = [pl.ds(0, middle), pl.ds(middle, count + extra - middle)]
    for j in range(blocks):
        for group in groups:
            value = state[group, block(j)]
            if j:
                value = value - times_exact(
                    (y_high[group, block(j - 1)], y_low[group, block(j - 1)]),
                    lower[block(j), block(j - 1)],
                    dot_nt,
                )
            value = times_pair(split(value), (inv_high[j], inv_low[j]), dot_nt)
            state[group, block(j)] = value
            y_high[group, block(j)], y_low[group, block(j)] = split(value)
            if 1 <= j < blocks - 1:
                done = pl.ds(0, BLOCK * j)
                state[group, block(j + 1)] = state[group, block(j + 1)] - times_exact(
                    (y_high[group, done], y_low[group, done]), lower[block(j + 1), done], dot_nt
                )
    for j in reversed(range(blocks)):
        for group in groups:
            value = state[group, block(j)]
            if j < blocks - 1:
                value = value - times_exact(
                    (out_high[group, block(j + 1)], out_low[group, block(j + 1)]),
                    lower[block(j + 1), block(j)],
                    dot_nn,
                )
            value = times_pair(split(value), (inv_high[j], inv_low[j]), dot_nn)
            out_high[group, block(j)], out_low[group, block(j)] = split(value)
            if 1 <= j < blocks - 1:
                done = pl.ds(BLOCK * (j + 1), BLOCK * (blocks - 1 - j))
                state[group, block(j - 1)] = state[group, block(j - 1)] - times_exact(
                    (out_high[group, done], out_low[group, done]), lower[done, block(j - 1)], dot_nn
                )


def solve(where, factor, train, query, extra):
    count, width = train.shape
    rows = count + extra
    blocks = width // BLOCK
    pair = jax.ShapeDtypeStruct((rows, width), BF16)
    train_pair = jax.ShapeDtypeStruct((count, width), BF16)
    return pl.pallas_call(
        solve_kernel,
        out_shape=(pair, pair, train_pair, train_pair),
        in_specs=[pl.BlockSpec(memory_space=pltpu.SMEM)] + [pl.BlockSpec(memory_space=pltpu.HBM)] * 3,
        out_specs=(pl.BlockSpec(memory_space=pltpu.VMEM),) * 4,
        scratch_shapes=[
            pltpu.VMEM((width, width), BF16),
            pltpu.VMEM((rows, width), F32),
            pltpu.VMEM((rows, width), BF16),
            pltpu.VMEM((rows, width), BF16),
            pltpu.VMEM((blocks, BLOCK, BLOCK), BF16),
            pltpu.VMEM((blocks, BLOCK, BLOCK), BF16),
            pltpu.SemaphoreType.DMA((2 * blocks + 1,)),
        ],
        compiler_params=pltpu.CompilerParams(vmem_limit_bytes=48 * 1024 * 1024),
        cost_estimate=pl.CostEstimate(
            flops=12 * rows * width * width, bytes_accessed=16 * 1024 * 1024, transcendentals=0
        ),
        name="solve",
    )(where, factor, train, query)


def local_kernel(
    scale, extra, where, *refs,
):
    pieces = refs[:-8]
    high, low, train_high, train_low, scores, send, keep, rows_buf = refs[-8:]
    piece_rows = pieces[0].shape[0]
    n_rows = piece_rows * len(pieces)
    for r, piece in enumerate(pieces):
        offset = pl.multiple_of((where[0] ^ r) * piece_rows, piece_rows)
        part_high, part_low = split(piece[...])
        rows_buf[pl.ds(offset, piece_rows), :] = part_high
        rows_buf[pl.ds(offset + n_rows, piece_rows), :] = part_low
    count = train_high.shape[0]
    weights_high, weights_low = high[0:count, :], low[0:count, :]
    both = dot_nt(rows_buf[...], weights_high)
    found = both[:n_rows] + both[n_rows:] + dot_nt(rows_buf[0:n_rows, :], weights_low)
    scores[...] = found
    pair = split(found * scale)
    n_pieces = 2 * send.shape[0]
    offset = pl.multiple_of(where[2], extra)
    factor = jnp.where(where[3] > 0, 0.5, 0.0).astype(F32)
    for place in range(n_pieces):
        at = place % (n_pieces // 2)
        out, order = (keep, where[1]) if place < n_pieces // 2 else (send, where[4])
        columns = pl.ds(pl.multiple_of((order ^ at) * BLOCK, BLOCK), BLOCK)
        out[at] = times_pair(pair, (train_high[:, columns], train_low[:, columns]), dot_nn)
        first = high[pl.ds(count, extra), columns].astype(F32) + low[pl.ds(count, extra), columns].astype(F32)
        out[at, pl.ds(offset, extra), :] = out[at, pl.ds(offset, extra), :] + factor * first


def local(where, pieces, high, low, train_high, train_low, extra, scale):
    n_rows = pieces[0].shape[0] * len(pieces)
    count, width = train_high.shape
    half = jax.ShapeDtypeStruct((width // BLOCK // 2, n_rows, BLOCK), F32)
    return pl.pallas_call(
        functools.partial(local_kernel, scale, extra),
        out_shape=(jax.ShapeDtypeStruct((n_rows, count), F32), half, half),
        in_specs=[pl.BlockSpec(memory_space=pltpu.SMEM)]
        + [pl.BlockSpec(memory_space=pltpu.VMEM)] * (len(pieces) + 4),
        out_specs=(pl.BlockSpec(memory_space=pltpu.VMEM),) * 3,
        scratch_shapes=[pltpu.VMEM((2 * n_rows, width), BF16)],
        compiler_params=pltpu.CompilerParams(vmem_limit_bytes=40 * 1024 * 1024),
        cost_estimate=pl.CostEstimate(
            flops=12 * n_rows * width * count, bytes_accessed=8 * 1024 * 1024, transcendentals=0
        ),
        name="local",
    )(where, *pieces, high, low, train_high, train_low)


def final_kernel(scale, where, scores, own, other, high, low, out):
    half = own.shape[0]
    count = out.shape[1]
    total = 2.0 * scores[...]
    for place in range(2 * half):
        at = place % half
        source, order = (own, where[1]) if place < half else (other, where[4])
        columns = pl.ds(pl.multiple_of((order ^ at) * BLOCK, BLOCK), BLOCK)
        total = total - times_pair(
            split(source[at]), (high[0:count, columns], low[0:count, columns]), dot_nt
        )
    out[...] = total * scale


def final(where, scores, own, other, high, low, scale):
    n_rows, count = scores.shape
    return pl.pallas_call(
        functools.partial(final_kernel, scale),
        out_shape=jax.ShapeDtypeStruct((n_rows, count), F32),
        in_specs=[pl.BlockSpec(memory_space=pltpu.SMEM)] + [pl.BlockSpec(memory_space=pltpu.VMEM)] * 5,
        out_specs=pl.BlockSpec(memory_space=pltpu.VMEM),
        compiler_params=pltpu.CompilerParams(vmem_limit_bytes=40 * 1024 * 1024),
        name="final",
    )(where, scores, own, other, high, low)


def bits(size):
    assert size & (size - 1) == 0
    return [1 << i for i in range(size.bit_length() - 1)]


def shards(queries, train_grads, factor):
    n_query, n_data = lax.axis_size("query"), lax.axis_size("dp")
    query_pos, data_pos = lax.axis_index("query"), lax.axis_index("dp")
    query_rows, width = queries.shape
    total_train = train_grads.shape[0] * n_data * n_query
    ranks = range(n_query * n_data)

    def swap(value, even, odd=None):
        odd = even if odd is None else odd
        return lax.ppermute(value, AXES, [(r, r ^ (odd if r & 1 else even)) for r in ranks])

    x_bits, z_bits = bits(n_query)[1:], [n_query * b for b in bits(n_data)]
    evens, odds = [], []
    for i in range(max(len(x_bits), len(z_bits))):
        evens += x_bits[i : i + 1] + z_bits[i : i + 1]
        odds += z_bits[i : i + 1] + x_bits[i : i + 1]
    steps = [(1, 1)] + list(zip(evens, odds))

    extra = max(16, query_rows // n_data)
    taken = data_pos * extra < query_rows
    start = jnp.where(taken, data_pos * extra, 0)
    rank = data_pos * n_query + query_pos
    n_pieces = width // BLOCK
    halvings = bits(n_pieces)[::-1]

    def order_of(rank):
        order = jnp.int32(0)
        for weight, (even, odd) in zip(halvings, steps):
            bit = jnp.where(rank & 1, odd, even)
            order = order + jnp.where((rank & bit) != 0, weight, 0)
        return order

    where = jnp.stack(
        [
            query_pos,
            order_of(rank),
            query_pos * query_rows + start,
            taken.astype(jnp.int32),
            order_of(rank ^ 1),
            start,
        ]
    )

    pieces = {0: queries}
    for bit in x_bits:
        pieces |= {r | bit: swap(piece, bit) for r, piece in pieces.items()}
    pieces[1] = swap(queries, 1)
    high, low, train_high, train_low = solve(where, factor, train_grads, queries, extra)
    far = [pieces[r] for r in range(2, n_query, 2)]
    far, high = lax.optimization_barrier((far, high))
    for r, piece in zip(range(2, n_query, 2), far):
        pieces[r | 1] = swap(piece, 1)
    pieces = [pieces[r] for r in range(n_query)]
    scores, send, keep = local(
        where, pieces, high, low, train_high, train_low, extra, 1.0 / total_train
    )

    got = swap(send, *steps[0])
    count = keep.shape[0]
    trail = [steps[0]]
    for step in steps[1:]:
        if count > 1 and len(trail) < len(halvings):
            count //= 2
            send, keep = keep[count:] + got[count:], keep[:count] + got[:count]
            trail.append(step)
            got = swap(send, *step)
        else:
            keep = keep + got
            got = swap(keep, *step)
    own = keep + got
    for step in reversed(trail[1:]):
        own = jnp.concatenate([own, swap(own, *step)], axis=0)
    other = swap(own, *trail[0])
    return final(where, scores, own, other, high, low, width**-0.5)


def solution(mesh):
    in_specs = (P(("groups", "query"), None), P(("groups", "dp", "query"), None), P("groups", None))
    out_specs = P("groups", ("dp", "query"))
    return jax.shard_map(shards, mesh=mesh, in_specs=in_specs, out_specs=out_specs, check_vma=False)
```

```python
import functools

import jax
import jax.numpy as jnp
from jax import lax
from jax.experimental import pallas as pl
from jax.experimental.pallas import tpu as pltpu
from jax.sharding import PartitionSpec as P

BLOCK = 256
HALF = 128
BASE = 16
AXES = ("dp", "query")
F32 = jnp.float32
BF16 = jnp.bfloat16


def split(value):
    high = value.astype(BF16)
    return high, (value - high.astype(F32)).astype(BF16)


def dot_nn(left, right):
    return lax.dot_general(left, right, (((1,), (0,)), ((), ())), preferred_element_type=F32)


def dot_nt(left, right):
    return lax.dot_general(left, right, (((1,), (1,)), ((), ())), preferred_element_type=F32)


def times_exact(left_pair, right, dot):
    rows = left_pair[0].shape[0]
    both = dot(jnp.concatenate(left_pair, axis=0), right)
    return both[:rows] + both[rows:]


def times_pair(left_pair, right_pair, dot):
    return times_exact(left_pair, right_pair[0], dot) + dot(left_pair[0], right_pair[1])


def invert_diagonals(lower, inv_high, inv_low, blocks):
    count = blocks * (BLOCK // HALF)
    row = lax.broadcasted_iota(jnp.int32, (HALF, HALF), 0)
    lane = lax.broadcasted_iota(jnp.int32, (HALF, HALF), 1)
    same = (row // BASE) == (lane // BASE)
    diagonals = [lower[pl.ds(HALF * g, HALF), pl.ds(HALF * g, HALF)].astype(F32) for g in range(count)]
    packed = []
    for diagonal in diagonals:
        kept = jnp.where(same, diagonal, 0.0)
        total = kept[0:BASE]
        for s in range(1, HALF // BASE):
            total = total + kept[s * BASE : (s + 1) * BASE]
        packed.append(total)
    packed = jnp.concatenate(packed, axis=0).astype(BF16)
    shape = (count, BASE, HALF)
    in_row = lax.broadcasted_iota(jnp.int32, shape, 1)
    in_lane = lax.broadcasted_iota(jnp.int32, shape, 2) % BASE
    solved = jnp.where(in_row == in_lane, 1.0, 0.0).astype(F32)
    for k in range(BASE):
        spread = jnp.where(row == (lane // BASE) * BASE + k, 1.0, 0.0).astype(BF16)
        column = dot_nn(packed, spread).reshape(shape)
        pivot_row = solved[:, k : k + 1, :] / column[:, k : k + 1, :]
        below = solved - column * pivot_row
        solved = jnp.where(in_row == k, pivot_row, jnp.where(in_row > k, below, solved))
    inverses = []
    for g in range(count):
        tiled = jnp.concatenate([solved[g]] * (HALF // BASE), axis=0)
        inverses.append(jnp.where(same, tiled, 0.0))
    size = BASE
    while size < HALF:
        part = (row // (2 * size) == lane // (2 * size)) & ((row // size) % 2 == 1) & ((lane // size) % 2 == 0)
        pairs = [split(x) for x in inverses]
        middles = []
        for g in range(count):
            below = jnp.where(part, diagonals[g], 0.0).astype(BF16)
            middles.append(
                dot_nn(jnp.concatenate([below, below], axis=1), jnp.concatenate(pairs[g], axis=0))
            )
        for g in range(count):
            mid_high, mid_low = split(middles[g])
            change = dot_nn(
                jnp.concatenate(pairs[g], axis=1), jnp.concatenate([mid_high, mid_high], axis=0)
            ) + dot_nn(pairs[g][0], mid_low)
            inverses[g] = inverses[g] - change
        size *= 2
    for j in range(blocks):
        upper, under = split(inverses[2 * j]), split(inverses[2 * j + 1])
        below = lower[pl.ds(BLOCK * j + HALF, HALF), pl.ds(BLOCK * j, HALF)]
        middle = dot_nn(jnp.concatenate([below, below], axis=1), jnp.concatenate(upper, axis=0))
        mid_high, mid_low = split(middle)
        corner = dot_nn(
            jnp.concatenate(under, axis=1), jnp.concatenate([mid_high, mid_high], axis=0)
        ) + dot_nn(under[0], mid_low)
        corner = split(-corner)
        zero = jnp.zeros((HALF, HALF), BF16)
        for part, out in ((0, inv_high), (1, inv_low)):
            out[j, 0:HALF, 0:HALF] = upper[part]
            out[j, 0:HALF, HALF:BLOCK] = zero
            out[j, HALF:BLOCK, 0:HALF] = corner[part]
            out[j, HALF:BLOCK, HALF:BLOCK] = under[part]


def solve_kernel(
    where, factor, train, query, out_high, out_low, train_high, train_low,
    lower, state, y_high, y_low, inv_high, inv_low, sems,
):
    blocks = factor.shape[0] // BLOCK
    count = train.shape[0]
    extra = state.shape[0] - count

    def block(j):
        return pl.ds(BLOCK * j, BLOCK)

    def fetch(source, target, at):
        return pltpu.make_async_copy(source, target, sems.at[at])

    diagonal = [
        fetch(factor.at[block(j), block(j)], lower.at[block(j), block(j)], j) for j in range(blocks)
    ]
    start = pl.multiple_of(where[1], extra)
    rest = [
        fetch(train, state.at[pl.ds(0, count), :], blocks),
        fetch(query.at[pl.ds(start, extra), :], state.at[pl.ds(count, extra), :], blocks + 1),
    ]
    for j in range(1, blocks):
        columns = pl.ds(0, BLOCK * j)
        rest.append(fetch(factor.at[block(j), columns], lower.at[block(j), columns], blocks + 1 + j))
    for copy in diagonal + rest:
        copy.start()
    for copy in diagonal:
        copy.wait()
    invert_diagonals(lower, inv_high, inv_low, blocks)
    for copy in rest:
        copy.wait()
    train_high[...], train_low[...] = split(state[0:count, :])

    middle = 16 * -(-(count + extra) // 32)
    groups = [pl.ds(0, middle), pl.ds(middle, count + extra - middle)]
    for j in range(blocks):
        for group in groups:
            value = state[group, block(j)]
            if j:
                value = value - times_exact(
                    (y_high[group, block(j - 1)], y_low[group, block(j - 1)]),
                    lower[block(j), block(j - 1)],
                    dot_nt,
                )
            value = times_pair(split(value), (inv_high[j], inv_low[j]), dot_nt)
            state[group, block(j)] = value
            y_high[group, block(j)], y_low[group, block(j)] = split(value)
            if 1 <= j < blocks - 1:
                done = pl.ds(0, BLOCK * j)
                state[group, block(j + 1)] = state[group, block(j + 1)] - times_exact(
                    (y_high[group, done], y_low[group, done]), lower[block(j + 1), done], dot_nt
                )
    for j in reversed(range(blocks)):
        for group in groups:
            value = state[group, block(j)]
            if j < blocks - 1:
                value = value - times_exact(
                    (out_high[group, block(j + 1)], out_low[group, block(j + 1)]),
                    lower[block(j + 1), block(j)],
                    dot_nn,
                )
            value = times_pair(split(value), (inv_high[j], inv_low[j]), dot_nn)
            out_high[group, block(j)], out_low[group, block(j)] = split(value)
            if 1 <= j < blocks - 1:
                done = pl.ds(BLOCK * (j + 1), BLOCK * (blocks - 1 - j))
                state[group, block(j - 1)] = state[group, block(j - 1)] - times_exact(
                    (out_high[group, done], out_low[group, done]), lower[done, block(j - 1)], dot_nn
                )


def solve(where, factor, train, query, extra):
    count, width = train.shape
    rows = count + extra
    blocks = width // BLOCK
    pair = jax.ShapeDtypeStruct((rows, width), BF16)
    train_pair = jax.ShapeDtypeStruct((count, width), BF16)
    return pl.pallas_call(
        solve_kernel,
        out_shape=(pair, pair, train_pair, train_pair),
        in_specs=[pl.BlockSpec(memory_space=pltpu.SMEM)] + [pl.BlockSpec(memory_space=pltpu.HBM)] * 3,
        out_specs=(pl.BlockSpec(memory_space=pltpu.VMEM),) * 4,
        scratch_shapes=[
            pltpu.VMEM((width, width), BF16),
            pltpu.VMEM((rows, width), F32),
            pltpu.VMEM((rows, width), BF16),
            pltpu.VMEM((rows, width), BF16),
            pltpu.VMEM((blocks, BLOCK, BLOCK), BF16),
            pltpu.VMEM((blocks, BLOCK, BLOCK), BF16),
            pltpu.SemaphoreType.DMA((2 * blocks + 1,)),
        ],
        compiler_params=pltpu.CompilerParams(vmem_limit_bytes=48 * 1024 * 1024),
        cost_estimate=pl.CostEstimate(
            flops=12 * rows * width * width, bytes_accessed=16 * 1024 * 1024, transcendentals=0
        ),
        name="solve",
    )(where, factor, train, query)


def product_terms(where, order_at, pair, high, low, train_high, train_low, out):
    n_rows, count = pair[0].shape
    extra = high.shape[0] - count
    half = n_rows // 2
    order, flip = where[order_at], where[order_at + 1]
    offset = pl.multiple_of(where[2] ^ (flip * half), extra)
    factor = jnp.where(where[3] > 0, 0.5, 0.0).astype(F32)
    for at in range(out.shape[0]):
        columns = pl.ds(pl.multiple_of((order ^ at) * BLOCK, BLOCK), BLOCK)
        found = times_pair(pair, (train_high[:, columns], train_low[:, columns]), dot_nn)
        for r in range(2):
            out[at, pl.ds(pl.multiple_of((r ^ flip) * half, half), half), :] = found[r * half : (r + 1) * half]
        first = high[pl.ds(count, extra), columns].astype(F32) + low[pl.ds(count, extra), columns].astype(F32)
        out[at, pl.ds(offset, extra), :] = out[at, pl.ds(offset, extra), :] + factor * first


def send_kernel(scale, where, *refs):
    pieces = refs[:-9]
    high, low, train_high, train_low, scores, pair_high, pair_low, send, rows_buf = refs[-9:]
    piece_rows = pieces[0].shape[0]
    n_rows, count = scores.shape
    for r, piece in enumerate(pieces):
        offset = pl.multiple_of((where[0] ^ r) * piece_rows, piece_rows)
        part_high, part_low = split(piece[...])
        rows_buf[pl.ds(offset, piece_rows), :] = part_high
        rows_buf[pl.ds(offset + n_rows, piece_rows), :] = part_low
    both = dot_nt(rows_buf[...], high[0:count, :])
    found = both[:n_rows] + both[n_rows:] + dot_nt(rows_buf[0:n_rows, :], low[0:count, :])
    scores[...] = found
    pair = split(found * scale)
    pair_high[...], pair_low[...] = pair
    product_terms(where, 6, pair, high, low, train_high, train_low, send)


def keep_kernel(where, pair_high, pair_low, high, low, train_high, train_low, keep):
    product_terms(where, 4, (pair_high[...], pair_low[...]), high, low, train_high, train_low, keep)


def on_vmem(kernel, out_shape, scratch, flops, name, where, *args):
    return pl.pallas_call(
        kernel,
        out_shape=out_shape,
        in_specs=[pl.BlockSpec(memory_space=pltpu.SMEM)] + [pl.BlockSpec(memory_space=pltpu.VMEM)] * len(args),
        out_specs=jax.tree.map(lambda _: pl.BlockSpec(memory_space=pltpu.VMEM), out_shape),
        scratch_shapes=scratch,
        compiler_params=pltpu.CompilerParams(vmem_limit_bytes=40 * 1024 * 1024),
        cost_estimate=pl.CostEstimate(flops=flops, bytes_accessed=4 * 1024 * 1024, transcendentals=0),
        name=name,
    )(where, *args)


def final_kernel(order_at, twice, scale, where, total, part, high, low, out):
    count = out.shape[1]
    half = out.shape[0] // 2
    order, flip = where[order_at], where[order_at + 1]
    result = total[...]
    if twice:
        result = result * 2.0
    for at in range(part.shape[0]):
        columns = pl.ds(pl.multiple_of((order ^ at) * BLOCK, BLOCK), BLOCK)
        rows = jnp.concatenate(
            [part[at, pl.ds(pl.multiple_of((r ^ flip) * half, half), half), :] for r in range(2)], axis=0
        )
        result = result - times_pair(split(rows), (high[0:count, columns], low[0:count, columns]), dot_nt)
    out[...] = result * scale


def bits(size):
    assert size & (size - 1) == 0
    return [1 << i for i in range(size.bit_length() - 1)]


def shards(queries, train_grads, factor):
    n_query, n_data = lax.axis_size("query"), lax.axis_size("dp")
    query_pos, data_pos = lax.axis_index("query"), lax.axis_index("dp")
    query_rows, width = queries.shape
    total_train = train_grads.shape[0] * n_data * n_query
    ranks = range(n_query * n_data)

    def swap(value, even, odd=None):
        odd = even if odd is None else odd
        return lax.ppermute(value, AXES, [(r, r ^ (odd if r & 1 else even)) for r in ranks])

    x_bits, z_bits = bits(n_query)[1:], [n_query * b for b in bits(n_data)]
    evens, odds = [], []
    for i in range(max(len(x_bits), len(z_bits))):
        evens += x_bits[i : i + 1] + z_bits[i : i + 1]
        odds += z_bits[i : i + 1] + x_bits[i : i + 1]
    steps = [(1, 1)] + list(zip(evens, odds))

    extra = max(16, query_rows // n_data)
    taken = data_pos * extra < query_rows
    start = jnp.where(taken, data_pos * extra, 0)
    rank = data_pos * n_query + query_pos
    n_pieces = width // BLOCK

    def order_of(rank):
        taken_bits = [(rank & jnp.where(rank & 1, odd, even)) != 0 for even, odd in steps[:3]]
        order = jnp.where(taken_bits[0], n_pieces // 2, 0) + jnp.where(taken_bits[1], n_pieces // 4, 0)
        return [order, taken_bits[2].astype(jnp.int32)]

    where = jnp.stack(
        [query_pos, start, query_pos * query_rows + start, taken.astype(jnp.int32)]
        + order_of(rank)
        + order_of(rank ^ 1)
    )

    pieces = {0: queries}
    for bit in x_bits:
        pieces |= {r | bit: swap(piece, bit) for r, piece in pieces.items()}
    pieces[1] = swap(queries, 1)
    high, low, train_high, train_low = solve(where, factor, train_grads, queries, extra)
    far = [pieces[r] for r in range(2, n_query, 2)]
    far, high = lax.optimization_barrier((far, high))
    for r, piece in zip(range(2, n_query, 2), far):
        pieces[r | 1] = swap(piece, 1)
    pieces = [pieces[r] for r in range(n_query)]

    n_rows, count = n_query * query_rows, train_grads.shape[0]
    scores_shape = jax.ShapeDtypeStruct((n_rows, count), F32)
    pair_shape = jax.ShapeDtypeStruct((n_rows, count), BF16)
    half_shape = jax.ShapeDtypeStruct((n_pieces // 2, n_rows, BLOCK), F32)
    operands = (high, low, train_high, train_low)
    flops = 3 * n_rows * width * count
    scores, pair_high, pair_low, send = on_vmem(
        functools.partial(send_kernel, 1.0 / total_train),
        (scores_shape, pair_shape, pair_shape, half_shape),
        [pltpu.VMEM((2 * n_rows, width), BF16)],
        3 * flops,
        "scores_and_send",
        where,
        *pieces,
        *operands,
    )
    got = swap(send, *steps[0])
    keep = on_vmem(keep_kernel, half_shape, [], flops, "keep", where, pair_high, pair_low, *operands)

    quarter, half = n_pieces // 4, n_rows // 2
    chunks = []
    for c in range(2):
        places = range(c * quarter // 2, (c + 1) * quarter // 2)
        first, last = places[0], places[-1] + 1
        mine = keep[first:last] + got[first:last]
        theirs = keep[quarter + first : quarter + last] + got[quarter + first : quarter + last]
        moved = swap(theirs, *steps[1])
        mine, theirs = mine[:, :half] + moved[:, :half], mine[:, half:] + moved[:, half:]
        mine = mine + swap(theirs, *steps[2])
        for step in steps[3:]:
            mine = mine + swap(mine, *step)
        mine = jnp.concatenate([mine, swap(mine, *steps[2])], axis=1)
        chunks.append((mine, swap(mine, *steps[1])))
    own = jnp.concatenate([chunks[0][0], chunks[1][0], chunks[0][1], chunks[1][1]], axis=0)
    other = swap(own, *steps[0])
    partial = on_vmem(
        functools.partial(final_kernel, 4, True, 1.0), scores_shape, [], flops, "own_columns", where, scores, own, high, low
    )
    return on_vmem(
        functools.partial(final_kernel, 6, False, width**-0.5),
        scores_shape, [], flops, "other_columns", where, partial, other, high, low,
    )


def solution(mesh):
    in_specs = (P(("groups", "query"), None), P(("groups", "dp", "query"), None), P("groups", None))
    out_specs = P("groups", ("dp", "query"))
    return jax.shard_map(shards, mesh=mesh, in_specs=in_specs, out_specs=out_specs, check_vma=False)
```

```python
import functools

import jax
import jax.numpy as jnp
from jax import lax
from jax.experimental import pallas as pl
from jax.experimental.pallas import tpu as pltpu
from jax.sharding import PartitionSpec as P

BLOCK = 256
HALF = 128
BASE = 16
AXES = ("dp", "query")
F32 = jnp.float32
BF16 = jnp.bfloat16


def split(value):
    high = value.astype(BF16)
    return high, (value - high.astype(F32)).astype(BF16)


def dot_nn(left, right):
    return lax.dot_general(left, right, (((1,), (0,)), ((), ())), preferred_element_type=F32)


def dot_nt(left, right):
    return lax.dot_general(left, right, (((1,), (1,)), ((), ())), preferred_element_type=F32)


def times_exact(left_pair, right, dot):
    rows = left_pair[0].shape[0]
    both = dot(jnp.concatenate(left_pair, axis=0), right)
    return both[:rows] + both[rows:]


def times_pair(left_pair, right_pair, dot):
    return times_exact(left_pair, right_pair[0], dot) + dot(left_pair[0], right_pair[1])


def invert_diagonals(lower, inv_high, inv_low, blocks):
    count = blocks * (BLOCK // HALF)
    row = lax.broadcasted_iota(jnp.int32, (HALF, HALF), 0)
    lane = lax.broadcasted_iota(jnp.int32, (HALF, HALF), 1)
    same = (row // BASE) == (lane // BASE)
    diagonals = [lower[pl.ds(HALF * g, HALF), pl.ds(HALF * g, HALF)].astype(F32) for g in range(count)]
    packed = []
    for diagonal in diagonals:
        kept = jnp.where(same, diagonal, 0.0)
        total = kept[0:BASE]
        for s in range(1, HALF // BASE):
            total = total + kept[s * BASE : (s + 1) * BASE]
        packed.append(total)
    packed = jnp.concatenate(packed, axis=0).astype(BF16)
    shape = (count, BASE, HALF)
    in_row = lax.broadcasted_iota(jnp.int32, shape, 1)
    in_lane = lax.broadcasted_iota(jnp.int32, shape, 2) % BASE
    solved = jnp.where(in_row == in_lane, 1.0, 0.0).astype(F32)
    for k in range(BASE):
        spread = jnp.where(row == (lane // BASE) * BASE + k, 1.0, 0.0).astype(BF16)
        column = dot_nn(packed, spread).reshape(shape)
        pivot_row = solved[:, k : k + 1, :] / column[:, k : k + 1, :]
        below = solved - column * pivot_row
        solved = jnp.where(in_row == k, pivot_row, jnp.where(in_row > k, below, solved))
    inverses = []
    for g in range(count):
        tiled = jnp.concatenate([solved[g]] * (HALF // BASE), axis=0)
        inverses.append(jnp.where(same, tiled, 0.0))
    size = BASE
    while size < HALF:
        part = (row // (2 * size) == lane // (2 * size)) & ((row // size) % 2 == 1) & ((lane // size) % 2 == 0)
        pairs = [split(x) for x in inverses]
        middles = []
        for g in range(count):
            below = jnp.where(part, diagonals[g], 0.0).astype(BF16)
            middles.append(
                dot_nn(jnp.concatenate([below, below], axis=1), jnp.concatenate(pairs[g], axis=0))
            )
        for g in range(count):
            mid_high, mid_low = split(middles[g])
            change = dot_nn(
                jnp.concatenate(pairs[g], axis=1), jnp.concatenate([mid_high, mid_high], axis=0)
            ) + dot_nn(pairs[g][0], mid_low)
            inverses[g] = inverses[g] - change
        size *= 2
    for j in range(blocks):
        upper, under = split(inverses[2 * j]), split(inverses[2 * j + 1])
        below = lower[pl.ds(BLOCK * j + HALF, HALF), pl.ds(BLOCK * j, HALF)]
        middle = dot_nn(jnp.concatenate([below, below], axis=1), jnp.concatenate(upper, axis=0))
        mid_high, mid_low = split(middle)
        corner = dot_nn(
            jnp.concatenate(under, axis=1), jnp.concatenate([mid_high, mid_high], axis=0)
        ) + dot_nn(under[0], mid_low)
        corner = split(-corner)
        zero = jnp.zeros((HALF, HALF), BF16)
        for part, out in ((0, inv_high), (1, inv_low)):
            out[j, 0:HALF, 0:HALF] = upper[part]
            out[j, 0:HALF, HALF:BLOCK] = zero
            out[j, HALF:BLOCK, 0:HALF] = corner[part]
            out[j, HALF:BLOCK, HALF:BLOCK] = under[part]


def solve_kernel(
    where, factor, train, query, out_high, out_low, train_high, train_low,
    lower, state, y_high, y_low, inv_high, inv_low, sems,
):
    blocks = factor.shape[0] // BLOCK
    count = train.shape[0]
    extra = state.shape[0] - count

    def block(j):
        return pl.ds(BLOCK * j, BLOCK)

    def fetch(source, target, at):
        return pltpu.make_async_copy(source, target, sems.at[at])

    diagonal = [
        fetch(factor.at[block(j), block(j)], lower.at[block(j), block(j)], j) for j in range(blocks)
    ]
    start = pl.multiple_of(where[1], extra)
    rest = [
        fetch(train, state.at[pl.ds(0, count), :], blocks),
        fetch(query.at[pl.ds(start, extra), :], state.at[pl.ds(count, extra), :], blocks + 1),
    ]
    for j in range(1, blocks):
        columns = pl.ds(0, BLOCK * j)
        rest.append(fetch(factor.at[block(j), columns], lower.at[block(j), columns], blocks + 1 + j))
    for copy in diagonal + rest:
        copy.start()
    for copy in diagonal:
        copy.wait()
    invert_diagonals(lower, inv_high, inv_low, blocks)
    for copy in rest:
        copy.wait()
    train_high[...], train_low[...] = split(state[0:count, :])

    middle = 16 * -(-(count + extra) // 32)
    groups = [pl.ds(0, middle), pl.ds(middle, count + extra - middle)]
    for j in range(blocks):
        for group in groups:
            value = state[group, block(j)]
            if j:
                value = value - times_exact(
                    (y_high[group, block(j - 1)], y_low[group, block(j - 1)]),
                    lower[block(j), block(j - 1)],
                    dot_nt,
                )
            value = times_pair(split(value), (inv_high[j], inv_low[j]), dot_nt)
            state[group, block(j)] = value
            y_high[group, block(j)], y_low[group, block(j)] = split(value)
            if 1 <= j < blocks - 1:
                done = pl.ds(0, BLOCK * j)
                state[group, block(j + 1)] = state[group, block(j + 1)] - times_exact(
                    (y_high[group, done], y_low[group, done]), lower[block(j + 1), done], dot_nt
                )
    for j in reversed(range(blocks)):
        for group in groups:
            value = state[group, block(j)]
            if j < blocks - 1:
                value = value - times_exact(
                    (out_high[group, block(j + 1)], out_low[group, block(j + 1)]),
                    lower[block(j + 1), block(j)],
                    dot_nn,
                )
            value = times_pair(split(value), (inv_high[j], inv_low[j]), dot_nn)
            out_high[group, block(j)], out_low[group, block(j)] = split(value)
            if 1 <= j < blocks - 1:
                done = pl.ds(BLOCK * (j + 1), BLOCK * (blocks - 1 - j))
                state[group, block(j - 1)] = state[group, block(j - 1)] - times_exact(
                    (out_high[group, done], out_low[group, done]), lower[done, block(j - 1)], dot_nn
                )


def solve(where, factor, train, query, extra):
    count, width = train.shape
    rows = count + extra
    blocks = width // BLOCK
    pair = jax.ShapeDtypeStruct((rows, width), BF16)
    train_pair = jax.ShapeDtypeStruct((count, width), BF16)
    return pl.pallas_call(
        solve_kernel,
        out_shape=(pair, pair, train_pair, train_pair),
        in_specs=[pl.BlockSpec(memory_space=pltpu.SMEM)] + [pl.BlockSpec(memory_space=pltpu.HBM)] * 3,
        out_specs=(pl.BlockSpec(memory_space=pltpu.VMEM),) * 4,
        scratch_shapes=[
            pltpu.VMEM((width, width), BF16),
            pltpu.VMEM((rows, width), F32),
            pltpu.VMEM((rows, width), BF16),
            pltpu.VMEM((rows, width), BF16),
            pltpu.VMEM((blocks, BLOCK, BLOCK), BF16),
            pltpu.VMEM((blocks, BLOCK, BLOCK), BF16),
            pltpu.SemaphoreType.DMA((2 * blocks + 1,)),
        ],
        compiler_params=pltpu.CompilerParams(vmem_limit_bytes=48 * 1024 * 1024),
        cost_estimate=pl.CostEstimate(
            flops=12 * rows * width * width, bytes_accessed=16 * 1024 * 1024, transcendentals=0
        ),
        name="solve",
    )(where, factor, train, query)


def product_terms(where, order_at, pair, high, low, train_high, train_low, out):
    n_rows, count = pair[0].shape
    extra = high.shape[0] - count
    half = n_rows // 2
    order, flip = where[order_at], where[order_at + 1]
    offset = pl.multiple_of(where[2] ^ (flip * half), extra)
    factor = jnp.where(where[3] > 0, 0.5, 0.0).astype(F32)
    for at in range(out.shape[0]):
        columns = pl.ds(pl.multiple_of((order ^ at) * BLOCK, BLOCK), BLOCK)
        found = times_pair(pair, (train_high[:, columns], train_low[:, columns]), dot_nn)
        for r in range(2):
            out[at, pl.ds(pl.multiple_of((r ^ flip) * half, half), half), :] = found[r * half : (r + 1) * half]
        first = high[pl.ds(count, extra), columns].astype(F32) + low[pl.ds(count, extra), columns].astype(F32)
        out[at, pl.ds(offset, extra), :] = out[at, pl.ds(offset, extra), :] + factor * first


def first_scores(pieces, high, low, rows_buf):
    piece_rows, count = pieces[0].shape[0], rows_buf.shape[0] // 2
    for r, piece in enumerate(pieces):
        part_high, part_low = split(piece[...])
        rows_buf[r * piece_rows : (r + 1) * piece_rows, :] = part_high
        rows_buf[count + r * piece_rows : count + (r + 1) * piece_rows, :] = part_low
    both = dot_nt(rows_buf[...], high)
    return both[:count] + both[count:] + dot_nt(rows_buf[0:count, :], low)


def near_kernel(where, *refs):
    high, low, out, rows_buf = refs[-4:]
    count = out.shape[1]
    out[...] = first_scores(refs[:-4], high[0:count, :], low[0:count, :], rows_buf)


def send_kernel(scale, near_places, where, *refs):
    pieces = refs[:-10]
    near, high, low, train_high, train_low, scores, pair_high, pair_low, send, rows_buf = refs[-10:]
    piece_rows = pieces[0].shape[0]
    count = scores.shape[1]
    far = first_scores(pieces, high[0:count, :], low[0:count, :], rows_buf)
    far_places = [r for r in range(len(pieces) + len(near_places)) if r not in near_places]
    for source, places in ((near[...], near_places), (far, far_places)):
        for i, r in enumerate(places):
            offset = pl.multiple_of((where[0] ^ r) * piece_rows, piece_rows)
            scores[pl.ds(offset, piece_rows), :] = source[i * piece_rows : (i + 1) * piece_rows]
    pair = split(scores[...] * scale)
    pair_high[...], pair_low[...] = pair
    product_terms(where, 6, pair, high, low, train_high, train_low, send)


def keep_kernel(where, pair_high, pair_low, high, low, train_high, train_low, keep):
    product_terms(where, 4, (pair_high[...], pair_low[...]), high, low, train_high, train_low, keep)


def on_vmem(kernel, out_shape, scratch, flops, name, where, *args):
    return pl.pallas_call(
        kernel,
        out_shape=out_shape,
        in_specs=[pl.BlockSpec(memory_space=pltpu.SMEM)] + [pl.BlockSpec(memory_space=pltpu.VMEM)] * len(args),
        out_specs=jax.tree.map(lambda _: pl.BlockSpec(memory_space=pltpu.VMEM), out_shape),
        scratch_shapes=scratch,
        compiler_params=pltpu.CompilerParams(vmem_limit_bytes=40 * 1024 * 1024),
        cost_estimate=pl.CostEstimate(flops=flops, bytes_accessed=4 * 1024 * 1024, transcendentals=0),
        name=name,
    )(where, *args)


def final_kernel(order_at, twice, scale, where, total, part, high, low, out):
    count = out.shape[1]
    half = out.shape[0] // 2
    order, flip = where[order_at], where[order_at + 1]
    result = total[...]
    if twice:
        result = result * 2.0
    for at in range(part.shape[0]):
        columns = pl.ds(pl.multiple_of((order ^ at) * BLOCK, BLOCK), BLOCK)
        rows = jnp.concatenate(
            [part[at, pl.ds(pl.multiple_of((r ^ flip) * half, half), half), :] for r in range(2)], axis=0
        )
        result = result - times_pair(split(rows), (high[0:count, columns], low[0:count, columns]), dot_nt)
    out[...] = result * scale


def bits(size):
    assert size & (size - 1) == 0
    return [1 << i for i in range(size.bit_length() - 1)]


def shards(queries, train_grads, factor):
    n_query, n_data = lax.axis_size("query"), lax.axis_size("dp")
    query_pos, data_pos = lax.axis_index("query"), lax.axis_index("dp")
    query_rows, width = queries.shape
    total_train = train_grads.shape[0] * n_data * n_query
    ranks = range(n_query * n_data)

    def swap(value, even, odd=None):
        odd = even if odd is None else odd
        return lax.ppermute(value, AXES, [(r, r ^ (odd if r & 1 else even)) for r in ranks])

    x_bits, z_bits = bits(n_query)[1:], [n_query * b for b in bits(n_data)]
    parity = {bit: bit for bit in [1] + x_bits + z_bits}
    if len(z_bits) > 1:
        parity[z_bits[0]] = z_bits[1] = z_bits[0] | z_bits[1]
    evens, odds = [], []
    for i in range(max(len(x_bits), len(z_bits))):
        evens += z_bits[i : i + 1] + x_bits[i : i + 1]
        odds += x_bits[i : i + 1] + z_bits[i : i + 1]
    steps = [(1, 1)] + list(zip(evens, odds))

    extra = max(16, query_rows // n_data)
    taken = data_pos * extra < query_rows
    start = jnp.where(taken, data_pos * extra, 0)
    rank = data_pos * n_query + query_pos
    n_pieces = width // BLOCK

    def order_of(rank):
        chosen = [rank & jnp.where(rank & 1, parity[odd], parity[even]) for even, odd in steps[:3]]
        chosen = [lax.population_count(bits_set) % 2 for bits_set in chosen]
        return [chosen[0] * (n_pieces // 2) + chosen[1] * (n_pieces // 4), chosen[2]]

    where = jnp.stack(
        [query_pos, start, query_pos * query_rows + start, taken.astype(jnp.int32)]
        + order_of(rank)
        + order_of(rank ^ 1)
    )

    pieces = {0: queries}
    for bit in x_bits:
        pieces |= {r | bit: swap(piece, bit) for r, piece in pieces.items()}
    pieces[1] = swap(queries, 1)
    high, low, train_high, train_low = solve(where, factor, train_grads, queries, extra)
    near_places = [0, 1] + list(range(2, n_query, 2))
    pieces, high = lax.optimization_barrier((pieces, high))
    far = [swap(pieces[r], 1) for r in range(2, n_query, 2)]
    near = on_vmem(
        near_kernel,
        jax.ShapeDtypeStruct((len(near_places) * query_rows, train_grads.shape[0]), F32),
        [pltpu.VMEM((2 * len(near_places) * query_rows, width), BF16)],
        6 * len(near_places) * query_rows * width * train_grads.shape[0],
        "near_scores",
        where,
        *[pieces[r] for r in near_places],
        high,
        low,
    )

    n_rows, count = n_query * query_rows, train_grads.shape[0]
    scores_shape = jax.ShapeDtypeStruct((n_rows, count), F32)
    pair_shape = jax.ShapeDtypeStruct((n_rows, count), BF16)
    half_shape = jax.ShapeDtypeStruct((n_pieces // 2, n_rows, BLOCK), F32)
    operands = (high, low, train_high, train_low)
    flops = 3 * n_rows * width * count
    scores, pair_high, pair_low, send = on_vmem(
        functools.partial(send_kernel, 1.0 / total_train, near_places),
        (scores_shape, pair_shape, pair_shape, half_shape),
        [pltpu.VMEM((2 * len(far) * query_rows, width), BF16)],
        2 * flops,
        "scores_and_send",
        where,
        *far,
        near,
        *operands,
    )
    got = swap(send, *steps[0])
    keep = on_vmem(keep_kernel, half_shape, [], flops, "keep", where, pair_high, pair_low, *operands)

    quarter, half = n_pieces // 4, n_rows // 2
    chunks = []
    for c in range(2):
        places = range(c * quarter // 2, (c + 1) * quarter // 2)
        first, last = places[0], places[-1] + 1
        mine = keep[first:last] + got[first:last]
        theirs = keep[quarter + first : quarter + last] + got[quarter + first : quarter + last]
        moved = swap(theirs, *steps[1])
        mine, theirs = mine[:, :half] + moved[:, :half], mine[:, half:] + moved[:, half:]
        mine = mine + swap(theirs, *steps[2])
        for step in steps[3:]:
            mine = mine + swap(mine, *step)
        mine = jnp.concatenate([mine, swap(mine, *steps[2])], axis=1)
        chunks.append((mine, swap(mine, *steps[1])))
    own = jnp.concatenate([chunks[0][0], chunks[1][0], chunks[0][1], chunks[1][1]], axis=0)
    other = swap(own, *steps[0])
    partial = on_vmem(
        functools.partial(final_kernel, 4, True, 1.0), scores_shape, [], flops, "own_columns", where, scores, own, high, low
    )
    return on_vmem(
        functools.partial(final_kernel, 6, False, width**-0.5),
        scores_shape, [], flops, "other_columns", where, partial, other, high, low,
    )


def solution(mesh):
    in_specs = (P(("groups", "query"), None), P(("groups", "dp", "query"), None), P("groups", None))
    out_specs = P("groups", ("dp", "query"))
    return jax.shard_map(shards, mesh=mesh, in_specs=in_specs, out_specs=out_specs, check_vma=False)
```

```python
import functools

import jax
import jax.numpy as jnp
from jax import lax
from jax.experimental import pallas as pl
from jax.experimental.pallas import tpu as pltpu
from jax.sharding import PartitionSpec as P

BLOCK = 256
HALF = 128
BASE = 16
AXES = ("dp", "query")
F32 = jnp.float32
BF16 = jnp.bfloat16


def split(value):
    high = value.astype(BF16)
    return high, (value - high.astype(F32)).astype(BF16)


def dot_nn(left, right):
    return lax.dot_general(left, right, (((1,), (0,)), ((), ())), preferred_element_type=F32)


def dot_nt(left, right):
    return lax.dot_general(left, right, (((1,), (1,)), ((), ())), preferred_element_type=F32)


def times_exact(left_pair, right, dot):
    rows = left_pair[0].shape[0]
    both = dot(jnp.concatenate(left_pair, axis=0), right)
    return both[:rows] + both[rows:]


def times_pair(left_pair, right_pair, dot):
    return times_exact(left_pair, right_pair[0], dot) + dot(left_pair[0], right_pair[1])


def invert_diagonals(lower, inv_high, inv_low, blocks):
    count = blocks * (BLOCK // HALF)
    row = lax.broadcasted_iota(jnp.int32, (HALF, HALF), 0)
    lane = lax.broadcasted_iota(jnp.int32, (HALF, HALF), 1)
    same = (row // BASE) == (lane // BASE)
    diagonals = [lower[pl.ds(HALF * g, HALF), pl.ds(HALF * g, HALF)].astype(F32) for g in range(count)]
    packed = []
    for diagonal in diagonals:
        kept = jnp.where(same, diagonal, 0.0)
        total = kept[0:BASE]
        for s in range(1, HALF // BASE):
            total = total + kept[s * BASE : (s + 1) * BASE]
        packed.append(total)
    packed = jnp.concatenate(packed, axis=0).astype(BF16)
    shape = (count, BASE, HALF)
    in_row = lax.broadcasted_iota(jnp.int32, shape, 1)
    in_lane = lax.broadcasted_iota(jnp.int32, shape, 2) % BASE
    solved = jnp.where(in_row == in_lane, 1.0, 0.0).astype(F32)
    for k in range(BASE):
        spread = jnp.where(row == (lane // BASE) * BASE + k, 1.0, 0.0).astype(BF16)
        column = dot_nn(packed, spread).reshape(shape)
        pivot_row = solved[:, k : k + 1, :] / column[:, k : k + 1, :]
        below = solved - column * pivot_row
        solved = jnp.where(in_row == k, pivot_row, jnp.where(in_row > k, below, solved))
    inverses = []
    for g in range(count):
        tiled = jnp.concatenate([solved[g]] * (HALF // BASE), axis=0)
        inverses.append(jnp.where(same, tiled, 0.0))
    size = BASE
    while size < HALF:
        part = (row // (2 * size) == lane // (2 * size)) & ((row // size) % 2 == 1) & ((lane // size) % 2 == 0)
        pairs = [split(x) for x in inverses]
        middles = []
        for g in range(count):
            below = jnp.where(part, diagonals[g], 0.0).astype(BF16)
            middles.append(
                dot_nn(jnp.concatenate([below, below], axis=1), jnp.concatenate(pairs[g], axis=0))
            )
        for g in range(count):
            mid_high, mid_low = split(middles[g])
            change = dot_nn(
                jnp.concatenate(pairs[g], axis=1), jnp.concatenate([mid_high, mid_high], axis=0)
            ) + dot_nn(pairs[g][0], mid_low)
            inverses[g] = inverses[g] - change
        size *= 2
    for j in range(blocks):
        upper, under = split(inverses[2 * j]), split(inverses[2 * j + 1])
        below = lower[pl.ds(BLOCK * j + HALF, HALF), pl.ds(BLOCK * j, HALF)]
        middle = dot_nn(jnp.concatenate([below, below], axis=1), jnp.concatenate(upper, axis=0))
        mid_high, mid_low = split(middle)
        corner = dot_nn(
            jnp.concatenate(under, axis=1), jnp.concatenate([mid_high, mid_high], axis=0)
        ) + dot_nn(under[0], mid_low)
        corner = split(-corner)
        zero = jnp.zeros((HALF, HALF), BF16)
        for part, out in ((0, inv_high), (1, inv_low)):
            out[j, 0:HALF, 0:HALF] = upper[part]
            out[j, 0:HALF, HALF:BLOCK] = zero
            out[j, HALF:BLOCK, 0:HALF] = corner[part]
            out[j, HALF:BLOCK, HALF:BLOCK] = under[part]


def solve_kernel(
    where, factor, train, query, out_high, out_low, train_high, train_low,
    lower, state, y_high, y_low, inv_high, inv_low, sems,
):
    blocks = factor.shape[0] // BLOCK
    count = train.shape[0]
    extra = state.shape[0] - count

    def block(j):
        return pl.ds(BLOCK * j, BLOCK)

    def fetch(source, target, at):
        return pltpu.make_async_copy(source, target, sems.at[at])

    diagonal = [
        fetch(factor.at[block(j), block(j)], lower.at[block(j), block(j)], j) for j in range(blocks)
    ]
    start = pl.multiple_of(where[1], extra)
    rest = [
        fetch(train, state.at[pl.ds(0, count), :], blocks),
        fetch(query.at[pl.ds(start, extra), :], state.at[pl.ds(count, extra), :], blocks + 1),
    ]
    for j in range(1, blocks):
        columns = pl.ds(0, BLOCK * j)
        rest.append(fetch(factor.at[block(j), columns], lower.at[block(j), columns], blocks + 1 + j))
    for copy in diagonal + rest:
        copy.start()
    for copy in diagonal:
        copy.wait()
    invert_diagonals(lower, inv_high, inv_low, blocks)
    for copy in rest:
        copy.wait()
    train_high[...], train_low[...] = split(state[0:count, :])

    middle = 16 * -(-(count + extra) // 32)
    groups = [pl.ds(0, middle), pl.ds(middle, count + extra - middle)]
    for j in range(blocks):
        for group in groups:
            value = state[group, block(j)]
            if j:
                value = value - times_exact(
                    (y_high[group, block(j - 1)], y_low[group, block(j - 1)]),
                    lower[block(j), block(j - 1)],
                    dot_nt,
                )
            value = times_pair(split(value), (inv_high[j], inv_low[j]), dot_nt)
            state[group, block(j)] = value
            y_high[group, block(j)], y_low[group, block(j)] = split(value)
            if 1 <= j < blocks - 1:
                done = pl.ds(0, BLOCK * j)
                state[group, block(j + 1)] = state[group, block(j + 1)] - times_exact(
                    (y_high[group, done], y_low[group, done]), lower[block(j + 1), done], dot_nt
                )
    for j in reversed(range(blocks)):
        for group in groups:
            value = state[group, block(j)]
            if j < blocks - 1:
                value = value - times_exact(
                    (out_high[group, block(j + 1)], out_low[group, block(j + 1)]),
                    lower[block(j + 1), block(j)],
                    dot_nn,
                )
            value = times_pair(split(value), (inv_high[j], inv_low[j]), dot_nn)
            out_high[group, block(j)], out_low[group, block(j)] = split(value)
            if 1 <= j < blocks - 1:
                done = pl.ds(BLOCK * (j + 1), BLOCK * (blocks - 1 - j))
                state[group, block(j - 1)] = state[group, block(j - 1)] - times_exact(
                    (out_high[group, done], out_low[group, done]), lower[done, block(j - 1)], dot_nn
                )


def solve(where, factor, train, query, extra):
    count, width = train.shape
    rows = count + extra
    blocks = width // BLOCK
    pair = jax.ShapeDtypeStruct((rows, width), BF16)
    train_pair = jax.ShapeDtypeStruct((count, width), BF16)
    return pl.pallas_call(
        solve_kernel,
        out_shape=(pair, pair, train_pair, train_pair),
        in_specs=[pl.BlockSpec(memory_space=pltpu.SMEM)] + [pl.BlockSpec(memory_space=pltpu.HBM)] * 3,
        out_specs=(pl.BlockSpec(memory_space=pltpu.VMEM),) * 4,
        scratch_shapes=[
            pltpu.VMEM((width, width), BF16),
            pltpu.VMEM((rows, width), F32),
            pltpu.VMEM((rows, width), BF16),
            pltpu.VMEM((rows, width), BF16),
            pltpu.VMEM((blocks, BLOCK, BLOCK), BF16),
            pltpu.VMEM((blocks, BLOCK, BLOCK), BF16),
            pltpu.SemaphoreType.DMA((2 * blocks + 1,)),
        ],
        compiler_params=pltpu.CompilerParams(vmem_limit_bytes=48 * 1024 * 1024),
        cost_estimate=pl.CostEstimate(
            flops=12 * rows * width * width, bytes_accessed=16 * 1024 * 1024, transcendentals=0
        ),
        name="solve",
    )(where, factor, train, query)


def product_terms(where, order_at, pair, high, low, train_high, train_low, out):
    n_rows, count = pair[0].shape
    extra = high.shape[0] - count
    half = n_rows // 2
    order, flip = where[order_at], where[order_at + 1]
    offset = pl.multiple_of(where[2] ^ (flip * half), extra)
    factor = jnp.where(where[3] > 0, 0.5, 0.0).astype(F32)
    for at in range(out.shape[0]):
        columns = pl.ds(pl.multiple_of((order ^ at) * BLOCK, BLOCK), BLOCK)
        found = times_pair(pair, (train_high[:, columns], train_low[:, columns]), dot_nn)
        for r in range(2):
            out[at, pl.ds(pl.multiple_of((r ^ flip) * half, half), half), :] = found[r * half : (r + 1) * half]
        first = high[pl.ds(count, extra), columns].astype(F32) + low[pl.ds(count, extra), columns].astype(F32)
        out[at, pl.ds(offset, extra), :] = out[at, pl.ds(offset, extra), :] + factor * first


def first_scores(pieces, high, low, rows_buf):
    piece_rows, count = pieces[0].shape[0], rows_buf.shape[0] // 2
    for r, piece in enumerate(pieces):
        part_high, part_low = split(piece[...])
        rows_buf[r * piece_rows : (r + 1) * piece_rows, :] = part_high
        rows_buf[count + r * piece_rows : count + (r + 1) * piece_rows, :] = part_low
    both = dot_nt(rows_buf[...], high)
    return both[:count] + both[count:] + dot_nt(rows_buf[0:count, :], low)


def near_kernel(where, *refs):
    high, low, out, rows_buf = refs[-4:]
    count = out.shape[1]
    out[...] = first_scores(refs[:-4], high[0:count, :], low[0:count, :], rows_buf)


def send_kernel(scale, near_places, where, *refs):
    pieces = refs[:-10]
    near, high, low, train_high, train_low, scores, pair_high, pair_low, send, rows_buf = refs[-10:]
    piece_rows = pieces[0].shape[0]
    count = scores.shape[1]
    far = first_scores(pieces, high[0:count, :], low[0:count, :], rows_buf)
    far_places = [r for r in range(len(pieces) + len(near_places)) if r not in near_places]
    for source, places in ((near[...], near_places), (far, far_places)):
        for i, r in enumerate(places):
            offset = pl.multiple_of((where[0] ^ r) * piece_rows, piece_rows)
            scores[pl.ds(offset, piece_rows), :] = source[i * piece_rows : (i + 1) * piece_rows]
    pair = split(scores[...] * scale)
    pair_high[...], pair_low[...] = pair
    product_terms(where, 6, pair, high, low, train_high, train_low, send)


def keep_kernel(where, pair_high, pair_low, high, low, train_high, train_low, keep):
    product_terms(where, 4, (pair_high[...], pair_low[...]), high, low, train_high, train_low, keep)


def on_vmem(kernel, out_shape, scratch, flops, name, where, *args):
    return pl.pallas_call(
        kernel,
        out_shape=out_shape,
        in_specs=[pl.BlockSpec(memory_space=pltpu.SMEM)] + [pl.BlockSpec(memory_space=pltpu.VMEM)] * len(args),
        out_specs=jax.tree.map(lambda _: pl.BlockSpec(memory_space=pltpu.VMEM), out_shape),
        scratch_shapes=scratch,
        compiler_params=pltpu.CompilerParams(vmem_limit_bytes=40 * 1024 * 1024),
        cost_estimate=pl.CostEstimate(flops=flops, bytes_accessed=4 * 1024 * 1024, transcendentals=0),
        name=name,
    )(where, *args)


def final_kernel(groups, twice, scale, where, total, *refs):
    parts = refs[:-3]
    high, low, out = refs[-3:]
    count = out.shape[1]
    half = out.shape[0] // 2
    result = total[...]
    if twice:
        result = result * 2.0
    for part, (order_at, places) in zip(parts, groups):
        order, flip = where[order_at], where[order_at + 1]
        for at, place in enumerate(places):
            columns = pl.ds(pl.multiple_of((order ^ place) * BLOCK, BLOCK), BLOCK)
            rows = jnp.concatenate(
                [part[at, pl.ds(pl.multiple_of((r ^ flip) * half, half), half), :] for r in range(2)], axis=0
            )
            result = result - times_pair(split(rows), (high[0:count, columns], low[0:count, columns]), dot_nt)
    out[...] = result * scale


def bits(size):
    assert size & (size - 1) == 0
    return [1 << i for i in range(size.bit_length() - 1)]


def shards(queries, train_grads, factor):
    n_query, n_data = lax.axis_size("query"), lax.axis_size("dp")
    query_pos, data_pos = lax.axis_index("query"), lax.axis_index("dp")
    query_rows, width = queries.shape
    total_train = train_grads.shape[0] * n_data * n_query
    ranks = range(n_query * n_data)

    def swap(value, even, odd=None):
        odd = even if odd is None else odd
        return lax.ppermute(value, AXES, [(r, r ^ (odd if r & 1 else even)) for r in ranks])

    x_bits, z_bits = bits(n_query)[1:], [n_query * b for b in bits(n_data)]
    parity = {bit: bit for bit in [1] + x_bits + z_bits}
    if len(z_bits) > 1:
        parity[z_bits[0]] = z_bits[1] = z_bits[0] | z_bits[1]
    evens, odds = [], []
    for i in range(max(len(x_bits), len(z_bits))):
        evens += z_bits[i : i + 1] + x_bits[i : i + 1]
        odds += x_bits[i : i + 1] + z_bits[i : i + 1]
    steps = [(1, 1)] + list(zip(evens, odds))

    extra = max(16, query_rows // n_data)
    taken = data_pos * extra < query_rows
    start = jnp.where(taken, data_pos * extra, 0)
    rank = data_pos * n_query + query_pos
    n_pieces = width // BLOCK

    def order_of(rank):
        chosen = [rank & jnp.where(rank & 1, parity[odd], parity[even]) for even, odd in steps[:3]]
        chosen = [lax.population_count(bits_set) % 2 for bits_set in chosen]
        return [chosen[0] * (n_pieces // 2) + chosen[1] * (n_pieces // 4), chosen[2]]

    where = jnp.stack(
        [query_pos, start, query_pos * query_rows + start, taken.astype(jnp.int32)]
        + order_of(rank)
        + order_of(rank ^ 1)
    )

    pieces = {0: queries}
    for bit in x_bits:
        pieces |= {r | bit: swap(piece, bit) for r, piece in pieces.items()}
    pieces[1] = swap(queries, 1)
    high, low, train_high, train_low = solve(where, factor, train_grads, queries, extra)
    near_places = [0, 1] + list(range(2, n_query, 2))
    pieces, high = lax.optimization_barrier((pieces, high))
    far = [swap(pieces[r], 1) for r in range(2, n_query, 2)]
    near = on_vmem(
        near_kernel,
        jax.ShapeDtypeStruct((len(near_places) * query_rows, train_grads.shape[0]), F32),
        [pltpu.VMEM((2 * len(near_places) * query_rows, width), BF16)],
        6 * len(near_places) * query_rows * width * train_grads.shape[0],
        "near_scores",
        where,
        *[pieces[r] for r in near_places],
        high,
        low,
    )

    n_rows, count = n_query * query_rows, train_grads.shape[0]
    scores_shape = jax.ShapeDtypeStruct((n_rows, count), F32)
    pair_shape = jax.ShapeDtypeStruct((n_rows, count), BF16)
    half_shape = jax.ShapeDtypeStruct((n_pieces // 2, n_rows, BLOCK), F32)
    operands = (high, low, train_high, train_low)
    flops = 3 * n_rows * width * count
    scores, pair_high, pair_low, send = on_vmem(
        functools.partial(send_kernel, 1.0 / total_train, near_places),
        (scores_shape, pair_shape, pair_shape, half_shape),
        [pltpu.VMEM((2 * len(far) * query_rows, width), BF16)],
        2 * flops,
        "scores_and_send",
        where,
        *far,
        near,
        *operands,
    )
    got = swap(send, *steps[0])
    keep = on_vmem(keep_kernel, half_shape, [], flops, "keep", where, pair_high, pair_low, *operands)

    quarter, half = n_pieces // 4, n_rows // 2
    chunks = []
    for c in range(2):
        places = range(c * quarter // 2, (c + 1) * quarter // 2)
        first, last = places[0], places[-1] + 1
        mine = keep[first:last] + got[first:last]
        theirs = keep[quarter + first : quarter + last] + got[quarter + first : quarter + last]
        moved = swap(theirs, *steps[1])
        mine, theirs = mine[:, :half] + moved[:, :half], mine[:, half:] + moved[:, half:]
        mine = mine + swap(theirs, *steps[2])
        for step in steps[3:]:
            mine = mine + swap(mine, *step)
        mine = jnp.concatenate([mine, swap(mine, *steps[2])], axis=1)
        mine = jnp.concatenate([mine, swap(mine, *steps[1])], axis=0)
        places = list(places) + [quarter + p for p in places]
        chunks.append((mine, places))

    def subtract(total, parts, groups, twice, scale, name):
        kernel = functools.partial(final_kernel, groups, twice, scale)
        count = sum(len(places) for _, places in groups)
        return on_vmem(
            kernel, scores_shape, [], 2 * flops * count // n_pieces, name, where, total, *parts, high, low
        )

    (own_a, places_a), (own_b, places_b) = chunks
    other_a = swap(own_a, *steps[0])
    total = subtract(scores, [own_a], [(4, places_a)], True, 1.0, "own_first")
    other_b = swap(own_b, *steps[0])
    total = subtract(total, [own_b, other_a], [(4, places_b), (6, places_a)], False, 1.0, "own_second")
    return subtract(total, [other_b], [(6, places_b)], False, width**-0.5, "other_second")


def solution(mesh):
    in_specs = (P(("groups", "query"), None), P(("groups", "dp", "query"), None), P("groups", None))
    out_specs = P("groups", ("dp", "query"))
    return jax.shard_map(shards, mesh=mesh, in_specs=in_specs, out_specs=out_specs, check_vma=False)
```

```python
import functools

import jax
import jax.numpy as jnp
from jax import lax
from jax.experimental import pallas as pl
from jax.experimental.pallas import tpu as pltpu
from jax.sharding import PartitionSpec as P

BLOCK = 256
HALF = 128
BASE = 16
AXES = ("dp", "query")
F32 = jnp.float32
BF16 = jnp.bfloat16


def split(value):
    high = value.astype(BF16)
    return high, (value - high.astype(F32)).astype(BF16)


def dot_nn(left, right):
    return lax.dot_general(left, right, (((1,), (0,)), ((), ())), preferred_element_type=F32)


def dot_nt(left, right):
    return lax.dot_general(left, right, (((1,), (1,)), ((), ())), preferred_element_type=F32)


def times_exact(left_pair, right, dot):
    rows = left_pair[0].shape[0]
    both = dot(jnp.concatenate(left_pair, axis=0), right)
    return both[:rows] + both[rows:]


def times_pair(left_pair, right_pair, dot):
    return times_exact(left_pair, right_pair[0], dot) + dot(left_pair[0], right_pair[1])


def invert_diagonals(lower, inv_high, inv_low, blocks):
    count = blocks * (BLOCK // HALF)
    row = lax.broadcasted_iota(jnp.int32, (HALF, HALF), 0)
    lane = lax.broadcasted_iota(jnp.int32, (HALF, HALF), 1)
    same = (row // BASE) == (lane // BASE)
    diagonals = [lower[pl.ds(HALF * g, HALF), pl.ds(HALF * g, HALF)].astype(F32) for g in range(count)]
    packed = []
    for diagonal in diagonals:
        kept = jnp.where(same, diagonal, 0.0)
        total = kept[0:BASE]
        for s in range(1, HALF // BASE):
            total = total + kept[s * BASE : (s + 1) * BASE]
        packed.append(total)
    packed = jnp.concatenate(packed, axis=0).astype(BF16)
    shape = (count, BASE, HALF)
    in_row = lax.broadcasted_iota(jnp.int32, shape, 1)
    in_lane = lax.broadcasted_iota(jnp.int32, shape, 2) % BASE
    solved = jnp.where(in_row == in_lane, 1.0, 0.0).astype(F32)
    for k in range(BASE):
        spread = jnp.where(row == (lane // BASE) * BASE + k, 1.0, 0.0).astype(BF16)
        column = dot_nn(packed, spread).reshape(shape)
        pivot_row = solved[:, k : k + 1, :] / column[:, k : k + 1, :]
        below = solved - column * pivot_row
        solved = jnp.where(in_row == k, pivot_row, jnp.where(in_row > k, below, solved))
    inverses = []
    for g in range(count):
        tiled = jnp.concatenate([solved[g]] * (HALF // BASE), axis=0)
        inverses.append(jnp.where(same, tiled, 0.0))
    size = BASE
    while size < HALF:
        part = (row // (2 * size) == lane // (2 * size)) & ((row // size) % 2 == 1) & ((lane // size) % 2 == 0)
        pairs = [split(x) for x in inverses]
        middles = []
        for g in range(count):
            below = jnp.where(part, diagonals[g], 0.0).astype(BF16)
            middles.append(
                dot_nn(jnp.concatenate([below, below], axis=1), jnp.concatenate(pairs[g], axis=0))
            )
        for g in range(count):
            mid_high, mid_low = split(middles[g])
            change = dot_nn(
                jnp.concatenate(pairs[g], axis=1), jnp.concatenate([mid_high, mid_high], axis=0)
            ) + dot_nn(pairs[g][0], mid_low)
            inverses[g] = inverses[g] - change
        size *= 2
    for j in range(blocks):
        upper, under = split(inverses[2 * j]), split(inverses[2 * j + 1])
        below = lower[pl.ds(BLOCK * j + HALF, HALF), pl.ds(BLOCK * j, HALF)]
        middle = dot_nn(jnp.concatenate([below, below], axis=1), jnp.concatenate(upper, axis=0))
        mid_high, mid_low = split(middle)
        corner = dot_nn(
            jnp.concatenate(under, axis=1), jnp.concatenate([mid_high, mid_high], axis=0)
        ) + dot_nn(under[0], mid_low)
        corner = split(-corner)
        zero = jnp.zeros((HALF, HALF), BF16)
        for part, out in ((0, inv_high), (1, inv_low)):
            out[j, 0:HALF, 0:HALF] = upper[part]
            out[j, 0:HALF, HALF:BLOCK] = zero
            out[j, HALF:BLOCK, 0:HALF] = corner[part]
            out[j, HALF:BLOCK, HALF:BLOCK] = under[part]


def solve_kernel(
    where, factor, train, query, out_high, out_low, train_high, train_low,
    lower, state, y_high, y_low, inv_high, inv_low, sems,
):
    blocks = factor.shape[0] // BLOCK
    count = train.shape[0]
    extra = state.shape[0] - count

    def block(j):
        return pl.ds(BLOCK * j, BLOCK)

    def fetch(source, target, at):
        return pltpu.make_async_copy(source, target, sems.at[at])

    diagonal = [
        fetch(factor.at[block(j), block(j)], lower.at[block(j), block(j)], j) for j in range(blocks)
    ]
    start = pl.multiple_of(where[1], extra)
    rest = [
        fetch(train, state.at[pl.ds(0, count), :], blocks),
        fetch(query.at[pl.ds(start, extra), :], state.at[pl.ds(count, extra), :], blocks + 1),
    ]
    for j in range(1, blocks):
        columns = pl.ds(0, BLOCK * j)
        rest.append(fetch(factor.at[block(j), columns], lower.at[block(j), columns], blocks + 1 + j))
    for copy in diagonal + rest:
        copy.start()
    for copy in diagonal:
        copy.wait()
    invert_diagonals(lower, inv_high, inv_low, blocks)
    for copy in rest:
        copy.wait()
    train_high[...], train_low[...] = split(state[0:count, :])

    middle = 16 * -(-(count + extra) // 32)
    groups = [pl.ds(0, middle), pl.ds(middle, count + extra - middle)]
    for j in range(blocks):
        for group in groups:
            value = state[group, block(j)]
            if j:
                value = value - times_exact(
                    (y_high[group, block(j - 1)], y_low[group, block(j - 1)]),
                    lower[block(j), block(j - 1)],
                    dot_nt,
                )
            value = times_pair(split(value), (inv_high[j], inv_low[j]), dot_nt)
            state[group, block(j)] = value
            y_high[group, block(j)], y_low[group, block(j)] = split(value)
            if 1 <= j < blocks - 1:
                done = pl.ds(0, BLOCK * j)
                state[group, block(j + 1)] = state[group, block(j + 1)] - times_exact(
                    (y_high[group, done], y_low[group, done]), lower[block(j + 1), done], dot_nt
                )
    for j in reversed(range(blocks)):
        for group in groups:
            value = state[group, block(j)]
            if j < blocks - 1:
                value = value - times_exact(
                    (out_high[group, block(j + 1)], out_low[group, block(j + 1)]),
                    lower[block(j + 1), block(j)],
                    dot_nn,
                )
            value = times_pair(split(value), (inv_high[j], inv_low[j]), dot_nn)
            out_high[group, block(j)], out_low[group, block(j)] = split(value)
            if 1 <= j < blocks - 1:
                done = pl.ds(BLOCK * (j + 1), BLOCK * (blocks - 1 - j))
                state[group, block(j - 1)] = state[group, block(j - 1)] - times_exact(
                    (out_high[group, done], out_low[group, done]), lower[done, block(j - 1)], dot_nn
                )


def solve(where, factor, train, query, extra):
    count, width = train.shape
    rows = count + extra
    blocks = width // BLOCK
    pair = jax.ShapeDtypeStruct((rows, width), BF16)
    train_pair = jax.ShapeDtypeStruct((count, width), BF16)
    return pl.pallas_call(
        solve_kernel,
        out_shape=(pair, pair, train_pair, train_pair),
        in_specs=[pl.BlockSpec(memory_space=pltpu.SMEM)] + [pl.BlockSpec(memory_space=pltpu.HBM)] * 3,
        out_specs=(pl.BlockSpec(memory_space=pltpu.VMEM),) * 4,
        scratch_shapes=[
            pltpu.VMEM((width, width), BF16),
            pltpu.VMEM((rows, width), F32),
            pltpu.VMEM((rows, width), BF16),
            pltpu.VMEM((rows, width), BF16),
            pltpu.VMEM((blocks, BLOCK, BLOCK), BF16),
            pltpu.VMEM((blocks, BLOCK, BLOCK), BF16),
            pltpu.SemaphoreType.DMA((2 * blocks + 1,)),
        ],
        compiler_params=pltpu.CompilerParams(vmem_limit_bytes=48 * 1024 * 1024),
        cost_estimate=pl.CostEstimate(
            flops=12 * rows * width * width, bytes_accessed=16 * 1024 * 1024, transcendentals=0
        ),
        name="solve",
    )(where, factor, train, query)


def product_terms(where, order_at, places, pair, high, low, train_high, train_low, out):
    n_rows, count = pair[0].shape
    extra = high.shape[0] - count
    half = n_rows // 2
    order, flip = where[order_at], where[order_at + 1]
    offset = pl.multiple_of(where[2] ^ (flip * half), extra)
    factor = jnp.where(where[3] > 0, 0.5, 0.0).astype(F32)
    for at, place in enumerate(places):
        columns = pl.ds(pl.multiple_of((order ^ place) * BLOCK, BLOCK), BLOCK)
        found = times_pair(pair, (train_high[:, columns], train_low[:, columns]), dot_nn)
        for r in range(2):
            out[at, pl.ds(pl.multiple_of((r ^ flip) * half, half), half), :] = found[r * half : (r + 1) * half]
        first = high[pl.ds(count, extra), columns].astype(F32) + low[pl.ds(count, extra), columns].astype(F32)
        out[at, pl.ds(offset, extra), :] = out[at, pl.ds(offset, extra), :] + factor * first


def first_scores(pieces, high, low, rows_buf):
    piece_rows, count = pieces[0].shape[0], rows_buf.shape[0] // 2
    for r, piece in enumerate(pieces):
        part_high, part_low = split(piece[...])
        rows_buf[r * piece_rows : (r + 1) * piece_rows, :] = part_high
        rows_buf[count + r * piece_rows : count + (r + 1) * piece_rows, :] = part_low
    both = dot_nt(rows_buf[...], high)
    return both[:count] + both[count:] + dot_nt(rows_buf[0:count, :], low)


def near_kernel(where, *refs):
    high, low, out, rows_buf = refs[-4:]
    count = out.shape[1]
    out[...] = first_scores(refs[:-4], high[0:count, :], low[0:count, :], rows_buf)


def send_kernel(scale, near_places, chunk_places, where, *refs):
    pieces = refs[:-10]
    near, high, low, train_high, train_low, scores, pair_high, pair_low, send, rows_buf = refs[-10:]
    piece_rows = pieces[0].shape[0]
    count = scores.shape[1]
    far = first_scores(pieces, high[0:count, :], low[0:count, :], rows_buf)
    far_places = [r for r in range(len(pieces) + len(near_places)) if r not in near_places]
    for source, places in ((near[...], near_places), (far, far_places)):
        for i, r in enumerate(places):
            offset = pl.multiple_of((where[0] ^ r) * piece_rows, piece_rows)
            scores[pl.ds(offset, piece_rows), :] = source[i * piece_rows : (i + 1) * piece_rows]
    pair = split(scores[...] * scale)
    pair_high[...], pair_low[...] = pair
    product_terms(where, 6, chunk_places, pair, high, low, train_high, train_low, send)


def terms_kernel(order_at, places, where, pair_high, pair_low, high, low, train_high, train_low, out):
    pair = (pair_high[...], pair_low[...])
    product_terms(where, order_at, places, pair, high, low, train_high, train_low, out)


def on_vmem(kernel, out_shape, scratch, flops, name, where, *args):
    return pl.pallas_call(
        kernel,
        out_shape=out_shape,
        in_specs=[pl.BlockSpec(memory_space=pltpu.SMEM)] + [pl.BlockSpec(memory_space=pltpu.VMEM)] * len(args),
        out_specs=jax.tree.map(lambda _: pl.BlockSpec(memory_space=pltpu.VMEM), out_shape),
        scratch_shapes=scratch,
        compiler_params=pltpu.CompilerParams(vmem_limit_bytes=40 * 1024 * 1024),
        cost_estimate=pl.CostEstimate(flops=flops, bytes_accessed=4 * 1024 * 1024, transcendentals=0),
        name=name,
    )(where, *args)


def final_kernel(groups, twice, scale, where, total, *refs):
    parts = refs[:-3]
    high, low, out = refs[-3:]
    count = out.shape[1]
    half = out.shape[0] // 2
    result = total[...]
    if twice:
        result = result * 2.0
    for part, (order_at, places) in zip(parts, groups):
        order, flip = where[order_at], where[order_at + 1]
        for at, place in enumerate(places):
            columns = pl.ds(pl.multiple_of((order ^ place) * BLOCK, BLOCK), BLOCK)
            rows = jnp.concatenate(
                [part[at, pl.ds(pl.multiple_of((r ^ flip) * half, half), half), :] for r in range(2)], axis=0
            )
            result = result - times_pair(split(rows), (high[0:count, columns], low[0:count, columns]), dot_nt)
    out[...] = result * scale


def bits(size):
    assert size & (size - 1) == 0
    return [1 << i for i in range(size.bit_length() - 1)]


def shards(queries, train_grads, factor):
    n_query, n_data = lax.axis_size("query"), lax.axis_size("dp")
    query_pos, data_pos = lax.axis_index("query"), lax.axis_index("dp")
    query_rows, width = queries.shape
    total_train = train_grads.shape[0] * n_data * n_query
    ranks = range(n_query * n_data)

    def swap(value, even, odd=None):
        odd = even if odd is None else odd
        return lax.ppermute(value, AXES, [(r, r ^ (odd if r & 1 else even)) for r in ranks])

    x_bits, z_bits = bits(n_query)[1:], [n_query * b for b in bits(n_data)]
    parity = {bit: bit for bit in [1] + x_bits + z_bits}
    if len(z_bits) > 1:
        parity[z_bits[0]] = z_bits[1] = z_bits[0] | z_bits[1]
    evens, odds = [], []
    for i in range(max(len(x_bits), len(z_bits))):
        evens += z_bits[i : i + 1] + x_bits[i : i + 1]
        odds += x_bits[i : i + 1] + z_bits[i : i + 1]
    steps = [(1, 1)] + list(zip(evens, odds))

    extra = max(16, query_rows // n_data)
    taken = data_pos * extra < query_rows
    start = jnp.where(taken, data_pos * extra, 0)
    rank = data_pos * n_query + query_pos
    n_pieces = width // BLOCK

    def order_of(rank):
        chosen = [rank & jnp.where(rank & 1, parity[odd], parity[even]) for even, odd in steps[:3]]
        chosen = [lax.population_count(bits_set) % 2 for bits_set in chosen]
        return [chosen[0] * (n_pieces // 2) + chosen[1] * (n_pieces // 4), chosen[2]]

    where = jnp.stack(
        [query_pos, start, query_pos * query_rows + start, taken.astype(jnp.int32)]
        + order_of(rank)
        + order_of(rank ^ 1)
    )

    pieces = {0: queries}
    for bit in x_bits:
        pieces |= {r | bit: swap(piece, bit) for r, piece in pieces.items()}
    pieces[1] = swap(queries, 1)
    high, low, train_high, train_low = solve(where, factor, train_grads, queries, extra)
    near_places = [0, 1] + list(range(2, n_query, 2))
    pieces, high = lax.optimization_barrier((pieces, high))
    far = [swap(pieces[r], 1) for r in range(2, n_query, 2)]
    near = on_vmem(
        near_kernel,
        jax.ShapeDtypeStruct((len(near_places) * query_rows, train_grads.shape[0]), F32),
        [pltpu.VMEM((2 * len(near_places) * query_rows, width), BF16)],
        6 * len(near_places) * query_rows * width * train_grads.shape[0],
        "near_scores",
        where,
        *[pieces[r] for r in near_places],
        high,
        low,
    )

    n_rows, count = n_query * query_rows, train_grads.shape[0]
    quarter, half = n_pieces // 4, n_rows // 2
    lead = quarter // 2
    places_of = [[q * quarter + c * lead + p for q in range(2) for p in range(lead)] for c in range(2)]
    scores_shape = jax.ShapeDtypeStruct((n_rows, count), F32)
    pair_shape = jax.ShapeDtypeStruct((n_rows, count), BF16)
    chunk_shape = jax.ShapeDtypeStruct((quarter, n_rows, BLOCK), F32)
    operands = (high, low, train_high, train_low)
    flops = 3 * n_rows * width * count
    scores, pair_high, pair_low, send = on_vmem(
        functools.partial(send_kernel, 1.0 / total_train, near_places, places_of[0]),
        (scores_shape, pair_shape, pair_shape, chunk_shape),
        [pltpu.VMEM((2 * len(far) * query_rows, width), BF16)],
        flops,
        "scores_and_send",
        where,
        *far,
        near,
        *operands,
    )

    def terms(order_at, places, name, high_part):
        kernel = functools.partial(terms_kernel, order_at, places)
        return on_vmem(kernel, chunk_shape, [], flops // 2, name, where, high_part, pair_low, *operands)

    got_first = swap(send, *steps[0])
    got_second = swap(terms(6, places_of[1], "send_second", pair_high), *steps[0])
    got = [got_first, got_second]
    keep = [terms(4, places_of[0], "keep_first", pair_high)]

    chunks = []
    for c in range(2):
        places = places_of[c]
        mine = keep[c][:lead] + got[c][:lead]
        theirs = keep[c][lead:] + got[c][lead:]
        if c == 0:
            theirs, later = lax.optimization_barrier((theirs, pair_high))
            keep.append(terms(4, places_of[1], "keep_second", later))
        moved = swap(theirs, *steps[1])
        mine, theirs = mine[:, :half] + moved[:, :half], mine[:, half:] + moved[:, half:]
        mine = mine + swap(theirs, *steps[2])
        for step in steps[3:]:
            mine = mine + swap(mine, *step)
        mine = jnp.concatenate([mine, swap(mine, *steps[2])], axis=1)
        mine = jnp.concatenate([mine, swap(mine, *steps[1])], axis=0)
        chunks.append((mine, places))

    def subtract(total, parts, groups, twice, scale, name):
        kernel = functools.partial(final_kernel, groups, twice, scale)
        count = sum(len(places) for _, places in groups)
        return on_vmem(
            kernel, scores_shape, [], 2 * flops * count // n_pieces, name, where, total, *parts, high, low
        )

    (own_a, places_a), (own_b, places_b) = chunks
    total = subtract(scores, [own_a], [(4, places_a)], True, 1.0, "own_first")
    own_a, total = lax.optimization_barrier((own_a, total))
    other_a = swap(own_a, *steps[0])
    other_b = swap(own_b, *steps[0])
    total = subtract(total, [own_b, other_a], [(4, places_b), (6, places_a)], False, 1.0, "own_second")
    return subtract(total, [other_b], [(6, places_b)], False, width**-0.5, "other_second")


def solution(mesh):
    in_specs = (P(("groups", "query"), None), P(("groups", "dp", "query"), None), P("groups", None))
    out_specs = P("groups", ("dp", "query"))
    return jax.shard_map(shards, mesh=mesh, in_specs=in_specs, out_specs=out_specs, check_vma=False)
```

```python
import functools

import jax
import jax.numpy as jnp
from jax import lax
from jax.experimental import pallas as pl
from jax.experimental.pallas import tpu as pltpu
from jax.sharding import PartitionSpec as P

BLOCK = 256
HALF = 128
BASE = 16
AXES = ("dp", "query")
F32 = jnp.float32
BF16 = jnp.bfloat16


def split(value):
    high = value.astype(BF16)
    return high, (value - high.astype(F32)).astype(BF16)


def dot_nn(left, right):
    return lax.dot_general(left, right, (((1,), (0,)), ((), ())), preferred_element_type=F32)


def dot_nt(left, right):
    return lax.dot_general(left, right, (((1,), (1,)), ((), ())), preferred_element_type=F32)


def times_exact(left_pair, right, dot):
    rows = left_pair[0].shape[0]
    both = dot(jnp.concatenate(left_pair, axis=0), right)
    return both[:rows] + both[rows:]


def times_pair(left_pair, right_pair, dot):
    return times_exact(left_pair, right_pair[0], dot) + dot(left_pair[0], right_pair[1])


def invert_diagonals(lower, inv_high, inv_low, blocks):
    count = blocks * (BLOCK // HALF)
    row = lax.broadcasted_iota(jnp.int32, (HALF, HALF), 0)
    lane = lax.broadcasted_iota(jnp.int32, (HALF, HALF), 1)
    same = (row // BASE) == (lane // BASE)
    diagonals = [lower[pl.ds(HALF * g, HALF), pl.ds(HALF * g, HALF)].astype(F32) for g in range(count)]
    packed = []
    for diagonal in diagonals:
        kept = jnp.where(same, diagonal, 0.0)
        total = kept[0:BASE]
        for s in range(1, HALF // BASE):
            total = total + kept[s * BASE : (s + 1) * BASE]
        packed.append(total)
    packed = jnp.concatenate(packed, axis=0).astype(BF16)
    shape = (count, BASE, HALF)
    in_row = lax.broadcasted_iota(jnp.int32, shape, 1)
    in_lane = lax.broadcasted_iota(jnp.int32, shape, 2) % BASE
    solved = jnp.where(in_row == in_lane, 1.0, 0.0).astype(F32)
    for k in range(BASE):
        spread = jnp.where(row == (lane // BASE) * BASE + k, 1.0, 0.0).astype(BF16)
        column = dot_nn(packed, spread).reshape(shape)
        pivot_row = solved[:, k : k + 1, :] / column[:, k : k + 1, :]
        below = solved - column * pivot_row
        solved = jnp.where(in_row == k, pivot_row, jnp.where(in_row > k, below, solved))
    inverses = []
    for g in range(count):
        tiled = jnp.concatenate([solved[g]] * (HALF // BASE), axis=0)
        inverses.append(jnp.where(same, tiled, 0.0))
    size = BASE
    while size < HALF:
        part = (row // (2 * size) == lane // (2 * size)) & ((row // size) % 2 == 1) & ((lane // size) % 2 == 0)
        pairs = [split(x) for x in inverses]
        middles = []
        for g in range(count):
            below = jnp.where(part, diagonals[g], 0.0).astype(BF16)
            middles.append(
                dot_nn(jnp.concatenate([below, below], axis=1), jnp.concatenate(pairs[g], axis=0))
            )
        for g in range(count):
            mid_high, mid_low = split(middles[g])
            change = dot_nn(
                jnp.concatenate(pairs[g], axis=1), jnp.concatenate([mid_high, mid_high], axis=0)
            ) + dot_nn(pairs[g][0], mid_low)
            inverses[g] = inverses[g] - change
        size *= 2
    for j in range(blocks):
        upper, under = split(inverses[2 * j]), split(inverses[2 * j + 1])
        below = lower[pl.ds(BLOCK * j + HALF, HALF), pl.ds(BLOCK * j, HALF)]
        middle = dot_nn(jnp.concatenate([below, below], axis=1), jnp.concatenate(upper, axis=0))
        mid_high, mid_low = split(middle)
        corner = dot_nn(
            jnp.concatenate(under, axis=1), jnp.concatenate([mid_high, mid_high], axis=0)
        ) + dot_nn(under[0], mid_low)
        corner = split(-corner)
        zero = jnp.zeros((HALF, HALF), BF16)
        for part, out in ((0, inv_high), (1, inv_low)):
            out[j, 0:HALF, 0:HALF] = upper[part]
            out[j, 0:HALF, HALF:BLOCK] = zero
            out[j, HALF:BLOCK, 0:HALF] = corner[part]
            out[j, HALF:BLOCK, HALF:BLOCK] = under[part]


def solve_kernel(
    where, factor, train, query, out_high, out_low, train_high, train_low,
    lower, state, y_high, y_low, inv_high, inv_low, sems,
):
    blocks = factor.shape[0] // BLOCK
    count = train.shape[0]
    extra = state.shape[0] - count

    def block(j):
        return pl.ds(BLOCK * j, BLOCK)

    def fetch(source, target, at):
        return pltpu.make_async_copy(source, target, sems.at[at])

    diagonal = [
        fetch(factor.at[block(j), block(j)], lower.at[block(j), block(j)], j) for j in range(blocks)
    ]
    start = pl.multiple_of(where[1], extra)
    rest = [
        fetch(train, state.at[pl.ds(0, count), :], blocks),
        fetch(query.at[pl.ds(start, extra), :], state.at[pl.ds(count, extra), :], blocks + 1),
    ]
    for j in range(1, blocks):
        columns = pl.ds(0, BLOCK * j)
        rest.append(fetch(factor.at[block(j), columns], lower.at[block(j), columns], blocks + 1 + j))
    for copy in diagonal + rest:
        copy.start()
    for copy in diagonal:
        copy.wait()
    invert_diagonals(lower, inv_high, inv_low, blocks)
    for copy in rest:
        copy.wait()
    train_high[...], train_low[...] = split(state[0:count, :])

    middle = 16 * -(-(count + extra) // 32)
    groups = [pl.ds(0, middle), pl.ds(middle, count + extra - middle)]
    for j in range(blocks):
        for group in groups:
            value = state[group, block(j)]
            if j:
                value = value - times_exact(
                    (y_high[group, block(j - 1)], y_low[group, block(j - 1)]),
                    lower[block(j), block(j - 1)],
                    dot_nt,
                )
            value = times_pair(split(value), (inv_high[j], inv_low[j]), dot_nt)
            state[group, block(j)] = value
            y_high[group, block(j)], y_low[group, block(j)] = split(value)
            if 1 <= j < blocks - 1:
                done = pl.ds(0, BLOCK * j)
                state[group, block(j + 1)] = state[group, block(j + 1)] - times_exact(
                    (y_high[group, done], y_low[group, done]), lower[block(j + 1), done], dot_nt
                )
    for j in reversed(range(blocks)):
        for group in groups:
            value = state[group, block(j)]
            if j < blocks - 1:
                value = value - times_exact(
                    (out_high[group, block(j + 1)], out_low[group, block(j + 1)]),
                    lower[block(j + 1), block(j)],
                    dot_nn,
                )
            value = times_pair(split(value), (inv_high[j], inv_low[j]), dot_nn)
            out_high[group, block(j)], out_low[group, block(j)] = split(value)
            if 1 <= j < blocks - 1:
                done = pl.ds(BLOCK * (j + 1), BLOCK * (blocks - 1 - j))
                state[group, block(j - 1)] = state[group, block(j - 1)] - times_exact(
                    (out_high[group, done], out_low[group, done]), lower[done, block(j - 1)], dot_nn
                )


def solve(where, factor, train, query, extra):
    count, width = train.shape
    rows = count + extra
    blocks = width // BLOCK
    pair = jax.ShapeDtypeStruct((rows, width), BF16)
    train_pair = jax.ShapeDtypeStruct((count, width), BF16)
    return pl.pallas_call(
        solve_kernel,
        out_shape=(pair, pair, train_pair, train_pair),
        in_specs=[pl.BlockSpec(memory_space=pltpu.SMEM)] + [pl.BlockSpec(memory_space=pltpu.HBM)] * 3,
        out_specs=(pl.BlockSpec(memory_space=pltpu.VMEM),) * 4,
        scratch_shapes=[
            pltpu.VMEM((width, width), BF16),
            pltpu.VMEM((rows, width), F32),
            pltpu.VMEM((rows, width), BF16),
            pltpu.VMEM((rows, width), BF16),
            pltpu.VMEM((blocks, BLOCK, BLOCK), BF16),
            pltpu.VMEM((blocks, BLOCK, BLOCK), BF16),
            pltpu.SemaphoreType.DMA((2 * blocks + 1,)),
        ],
        compiler_params=pltpu.CompilerParams(vmem_limit_bytes=48 * 1024 * 1024),
        cost_estimate=pl.CostEstimate(
            flops=12 * rows * width * width, bytes_accessed=16 * 1024 * 1024, transcendentals=0
        ),
        name="solve",
    )(where, factor, train, query)


def product_terms(where, order_at, places, pair, high, low, train_high, train_low, out):
    n_rows, count = pair[0].shape
    extra = high.shape[0] - count
    half = n_rows // 2
    order, flip = where[order_at], where[order_at + 1]
    offset = pl.multiple_of(where[2] ^ (flip * half), extra)
    factor = jnp.where(where[3] > 0, 0.5, 0.0).astype(F32)
    for at, place in enumerate(places):
        columns = pl.ds(pl.multiple_of((order ^ place) * BLOCK, BLOCK), BLOCK)
        found = times_pair(pair, (train_high[:, columns], train_low[:, columns]), dot_nn)
        for r in range(2):
            out[at, pl.ds(pl.multiple_of((r ^ flip) * half, half), half), :] = found[r * half : (r + 1) * half]
        first = high[pl.ds(count, extra), columns].astype(F32) + low[pl.ds(count, extra), columns].astype(F32)
        out[at, pl.ds(offset, extra), :] = out[at, pl.ds(offset, extra), :] + factor * first


def first_scores(pieces, high, low, rows_buf):
    piece_rows, count = pieces[0].shape[0], rows_buf.shape[0] // 2
    for r, piece in enumerate(pieces):
        part_high, part_low = split(piece[...])
        rows_buf[r * piece_rows : (r + 1) * piece_rows, :] = part_high
        rows_buf[count + r * piece_rows : count + (r + 1) * piece_rows, :] = part_low
    both = dot_nt(rows_buf[...], high)
    return both[:count] + both[count:] + dot_nt(rows_buf[0:count, :], low)


def near_kernel(where, *refs):
    high, low, out, rows_buf = refs[-4:]
    count = out.shape[1]
    out[...] = first_scores(refs[:-4], high[0:count, :], low[0:count, :], rows_buf)


def send_kernel(scale, near_places, chunk_places, where, *refs):
    pieces = refs[:-10]
    near, high, low, train_high, train_low, scores, pair_high, pair_low, send, rows_buf = refs[-10:]
    piece_rows = pieces[0].shape[0]
    count = scores.shape[1]
    far = first_scores(pieces, high[0:count, :], low[0:count, :], rows_buf)
    far_places = [r for r in range(len(pieces) + len(near_places)) if r not in near_places]
    for source, places in ((near[...], near_places), (far, far_places)):
        for i, r in enumerate(places):
            offset = pl.multiple_of((where[0] ^ r) * piece_rows, piece_rows)
            scores[pl.ds(offset, piece_rows), :] = source[i * piece_rows : (i + 1) * piece_rows]
    pair = split(scores[...] * scale)
    pair_high[...], pair_low[...] = pair
    product_terms(where, 6, chunk_places, pair, high, low, train_high, train_low, send)


def terms_kernel(order_at, places, where, pair_high, pair_low, high, low, train_high, train_low, out):
    pair = (pair_high[...], pair_low[...])
    product_terms(where, order_at, places, pair, high, low, train_high, train_low, out)


def on_vmem(kernel, out_shape, scratch, flops, name, where, *args):
    return pl.pallas_call(
        kernel,
        out_shape=out_shape,
        in_specs=[pl.BlockSpec(memory_space=pltpu.SMEM)] + [pl.BlockSpec(memory_space=pltpu.VMEM)] * len(args),
        out_specs=jax.tree.map(lambda _: pl.BlockSpec(memory_space=pltpu.VMEM), out_shape),
        scratch_shapes=scratch,
        compiler_params=pltpu.CompilerParams(vmem_limit_bytes=40 * 1024 * 1024),
        cost_estimate=pl.CostEstimate(flops=flops, bytes_accessed=4 * 1024 * 1024, transcendentals=0),
        name=name,
    )(where, *args)


def final_kernel(groups, twice, scale, where, total, *refs):
    parts = refs[:-3]
    high, low, out = refs[-3:]
    count = out.shape[1]
    half = out.shape[0] // 2
    result = total[...]
    if twice:
        result = result * 2.0
    for part, (order_at, places) in zip(parts, groups):
        order, flip = where[order_at], where[order_at + 1]
        for at, place in enumerate(places):
            columns = pl.ds(pl.multiple_of((order ^ place) * BLOCK, BLOCK), BLOCK)
            rows = jnp.concatenate(
                [part[at, pl.ds(pl.multiple_of((r ^ flip) * half, half), half), :] for r in range(2)], axis=0
            )
            result = result - times_pair(split(rows), (high[0:count, columns], low[0:count, columns]), dot_nt)
    out[...] = result * scale


def bits(size):
    assert size & (size - 1) == 0
    return [1 << i for i in range(size.bit_length() - 1)]


def shards(queries, train_grads, factor):
    n_query, n_data = lax.axis_size("query"), lax.axis_size("dp")
    query_pos, data_pos = lax.axis_index("query"), lax.axis_index("dp")
    query_rows, width = queries.shape
    total_train = train_grads.shape[0] * n_data * n_query
    ranks = range(n_query * n_data)

    def swap(value, even, odd=None):
        odd = even if odd is None else odd
        return lax.ppermute(value, AXES, [(r, r ^ (odd if r & 1 else even)) for r in ranks])

    x_bits, z_bits = bits(n_query)[1:], [n_query * b for b in bits(n_data)]
    parity = {bit: bit for bit in [1] + x_bits + z_bits}
    if len(z_bits) > 1:
        parity[z_bits[0]] = z_bits[1] = z_bits[0] | z_bits[1]
    evens, odds = [], []
    for i in range(max(len(x_bits), len(z_bits))):
        evens += z_bits[i : i + 1] + x_bits[i : i + 1]
        odds += x_bits[i : i + 1] + z_bits[i : i + 1]
    steps = [(1, 1)] + list(zip(evens, odds))

    extra = max(16, query_rows // n_data)
    taken = data_pos * extra < query_rows
    start = jnp.where(taken, data_pos * extra, 0)
    rank = data_pos * n_query + query_pos
    n_pieces = width // BLOCK

    def order_of(rank):
        chosen = [rank & jnp.where(rank & 1, parity[odd], parity[even]) for even, odd in steps[:3]]
        chosen = [lax.population_count(bits_set) % 2 for bits_set in chosen]
        return [chosen[0] * (n_pieces // 2) + chosen[1] * (n_pieces // 4), chosen[2]]

    where = jnp.stack(
        [query_pos, start, query_pos * query_rows + start, taken.astype(jnp.int32)]
        + order_of(rank)
        + order_of(rank ^ 1)
    )

    pieces = {0: queries}
    for bit in x_bits:
        pieces |= {r | bit: swap(piece, bit) for r, piece in pieces.items()}
    high, low, train_high, train_low = solve(where, factor, train_grads, queries, extra)
    near_places = list(range(0, n_query, 2))
    pieces, high = lax.optimization_barrier((pieces, high))
    far = [swap(pieces[r], 1) for r in near_places]
    near = on_vmem(
        near_kernel,
        jax.ShapeDtypeStruct((len(near_places) * query_rows, train_grads.shape[0]), F32),
        [pltpu.VMEM((2 * len(near_places) * query_rows, width), BF16)],
        6 * len(near_places) * query_rows * width * train_grads.shape[0],
        "near_scores",
        where,
        *[pieces[r] for r in near_places],
        high,
        low,
    )

    n_rows, count = n_query * query_rows, train_grads.shape[0]
    quarter, half = n_pieces // 4, n_rows // 2
    lead = quarter // 2
    places_of = [[q * quarter + c * lead + p for q in range(2) for p in range(lead)] for c in range(2)]
    scores_shape = jax.ShapeDtypeStruct((n_rows, count), F32)
    pair_shape = jax.ShapeDtypeStruct((n_rows, count), BF16)
    chunk_shape = jax.ShapeDtypeStruct((quarter, n_rows, BLOCK), F32)
    operands = (high, low, train_high, train_low)
    flops = 3 * n_rows * width * count
    scores, pair_high, pair_low, send = on_vmem(
        functools.partial(send_kernel, 1.0 / total_train, near_places, places_of[0]),
        (scores_shape, pair_shape, pair_shape, chunk_shape),
        [pltpu.VMEM((2 * len(far) * query_rows, width), BF16)],
        flops,
        "scores_and_send",
        where,
        *far,
        near,
        *operands,
    )

    def terms(order_at, places, name, high_part):
        kernel = functools.partial(terms_kernel, order_at, places)
        return on_vmem(kernel, chunk_shape, [], flops // 2, name, where, high_part, pair_low, *operands)

    got_first = swap(send, *steps[0])
    got_second = swap(terms(6, places_of[1], "send_second", pair_high), *steps[0])
    got = [got_first, got_second]
    keep = [terms(4, places_of[0], "keep_first", pair_high)]

    chunks = []
    for c in range(2):
        places = places_of[c]
        mine = keep[c][:lead] + got[c][:lead]
        theirs = keep[c][lead:] + got[c][lead:]
        if c == 0:
            theirs, later = lax.optimization_barrier((theirs, pair_high))
            keep.append(terms(4, places_of[1], "keep_second", later))
        moved = swap(theirs, *steps[1])
        mine, theirs = mine[:, :half] + moved[:, :half], mine[:, half:] + moved[:, half:]
        mine = mine + swap(theirs, *steps[2])
        for step in steps[3:]:
            mine = mine + swap(mine, *step)
        mine = jnp.concatenate([mine, swap(mine, *steps[2])], axis=1)
        mine = jnp.concatenate([mine, swap(mine, *steps[1])], axis=0)
        chunks.append((mine, places))

    def subtract(total, parts, groups, twice, scale, name):
        kernel = functools.partial(final_kernel, groups, twice, scale)
        count = sum(len(places) for _, places in groups)
        return on_vmem(
            kernel, scores_shape, [], 2 * flops * count // n_pieces, name, where, total, *parts, high, low
        )

    (own_a, places_a), (own_b, places_b) = chunks
    total = subtract(scores, [own_a], [(4, places_a)], True, 1.0, "own_first")
    own_a, total = lax.optimization_barrier((own_a, total))
    other_a = swap(own_a, *steps[0])
    other_b = swap(own_b, *steps[0])
    total = subtract(total, [own_b, other_a], [(4, places_b), (6, places_a)], False, 1.0, "own_second")
    return subtract(total, [other_b], [(6, places_b)], False, width**-0.5, "other_second")


def solution(mesh):
    in_specs = (P(("groups", "query"), None), P(("groups", "dp", "query"), None), P("groups", None))
    out_specs = P("groups", ("dp", "query"))
    return jax.shard_map(shards, mesh=mesh, in_specs=in_specs, out_specs=out_specs, check_vma=False)
```

```python
import functools

import jax
import jax.numpy as jnp
from jax import lax
from jax.experimental import pallas as pl
from jax.experimental.pallas import tpu as pltpu
from jax.sharding import PartitionSpec as P

BLOCK = 256
HALF = 128
BASE = 16
AXES = ("dp", "query")
F32 = jnp.float32
BF16 = jnp.bfloat16


def split(value):
    high = value.astype(BF16)
    return high, (value - high.astype(F32)).astype(BF16)


def dot_nn(left, right):
    return lax.dot_general(left, right, (((1,), (0,)), ((), ())), preferred_element_type=F32)


def dot_nt(left, right):
    return lax.dot_general(left, right, (((1,), (1,)), ((), ())), preferred_element_type=F32)


def times_exact(left_pair, right, dot):
    rows = left_pair[0].shape[0]
    both = dot(jnp.concatenate(left_pair, axis=0), right)
    return both[:rows] + both[rows:]


def times_pair(left_pair, right_pair, dot):
    return times_exact(left_pair, right_pair[0], dot) + dot(left_pair[0], right_pair[1])


def invert_diagonals(lower, inv_high, inv_low, blocks):
    count = blocks * (BLOCK // HALF)
    row = lax.broadcasted_iota(jnp.int32, (HALF, HALF), 0)
    lane = lax.broadcasted_iota(jnp.int32, (HALF, HALF), 1)
    same = (row // BASE) == (lane // BASE)
    diagonals = [lower[pl.ds(HALF * g, HALF), pl.ds(HALF * g, HALF)].astype(F32) for g in range(count)]
    packed = []
    for diagonal in diagonals:
        kept = jnp.where(same, diagonal, 0.0)
        total = kept[0:BASE]
        for s in range(1, HALF // BASE):
            total = total + kept[s * BASE : (s + 1) * BASE]
        packed.append(total)
    packed = jnp.concatenate(packed, axis=0).astype(BF16)
    shape = (count, BASE, HALF)
    in_row = lax.broadcasted_iota(jnp.int32, shape, 1)
    in_lane = lax.broadcasted_iota(jnp.int32, shape, 2) % BASE
    solved = jnp.where(in_row == in_lane, 1.0, 0.0).astype(F32)
    for k in range(BASE):
        spread = jnp.where(row == (lane // BASE) * BASE + k, 1.0, 0.0).astype(BF16)
        column = dot_nn(packed, spread).reshape(shape)
        pivot_row = solved[:, k : k + 1, :] / column[:, k : k + 1, :]
        below = solved - column * pivot_row
        solved = jnp.where(in_row == k, pivot_row, jnp.where(in_row > k, below, solved))
    inverses = []
    for g in range(count):
        tiled = jnp.concatenate([solved[g]] * (HALF // BASE), axis=0)
        inverses.append(jnp.where(same, tiled, 0.0))
    size = BASE
    while size < HALF:
        part = (row // (2 * size) == lane // (2 * size)) & ((row // size) % 2 == 1) & ((lane // size) % 2 == 0)
        pairs = [split(x) for x in inverses]
        middles = []
        for g in range(count):
            below = jnp.where(part, diagonals[g], 0.0).astype(BF16)
            middles.append(
                dot_nn(jnp.concatenate([below, below], axis=1), jnp.concatenate(pairs[g], axis=0))
            )
        for g in range(count):
            mid_high, mid_low = split(middles[g])
            change = dot_nn(
                jnp.concatenate(pairs[g], axis=1), jnp.concatenate([mid_high, mid_high], axis=0)
            ) + dot_nn(pairs[g][0], mid_low)
            inverses[g] = inverses[g] - change
        size *= 2
    for j in range(blocks):
        upper, under = split(inverses[2 * j]), split(inverses[2 * j + 1])
        below = lower[pl.ds(BLOCK * j + HALF, HALF), pl.ds(BLOCK * j, HALF)]
        middle = dot_nn(jnp.concatenate([below, below], axis=1), jnp.concatenate(upper, axis=0))
        mid_high, mid_low = split(middle)
        corner = dot_nn(
            jnp.concatenate(under, axis=1), jnp.concatenate([mid_high, mid_high], axis=0)
        ) + dot_nn(under[0], mid_low)
        corner = split(-corner)
        zero = jnp.zeros((HALF, HALF), BF16)
        for part, out in ((0, inv_high), (1, inv_low)):
            out[j, 0:HALF, 0:HALF] = upper[part]
            out[j, 0:HALF, HALF:BLOCK] = zero
            out[j, HALF:BLOCK, 0:HALF] = corner[part]
            out[j, HALF:BLOCK, HALF:BLOCK] = under[part]


def solve_kernel(
    where, factor, train, query, out_high, out_low, train_high, train_low,
    lower, state, y_high, y_low, inv_high, inv_low, sems,
):
    blocks = factor.shape[0] // BLOCK
    count = train.shape[0]
    extra = state.shape[0] - count

    def block(j):
        return pl.ds(BLOCK * j, BLOCK)

    def fetch(source, target, at):
        return pltpu.make_async_copy(source, target, sems.at[at])

    diagonal = [
        fetch(factor.at[block(j), block(j)], lower.at[block(j), block(j)], j) for j in range(blocks)
    ]
    start = pl.multiple_of(where[1], extra)
    rest = [
        fetch(train, state.at[pl.ds(0, count), :], blocks),
        fetch(query.at[pl.ds(start, extra), :], state.at[pl.ds(count, extra), :], blocks + 1),
    ]
    for j in range(1, blocks):
        columns = pl.ds(0, BLOCK * j)
        rest.append(fetch(factor.at[block(j), columns], lower.at[block(j), columns], blocks + 1 + j))
    for copy in diagonal + rest:
        copy.start()
    for copy in diagonal:
        copy.wait()
    invert_diagonals(lower, inv_high, inv_low, blocks)
    for copy in rest:
        copy.wait()
    train_high[...], train_low[...] = split(state[0:count, :])

    middle = 16 * -(-(count + extra) // 32)
    groups = [pl.ds(0, middle), pl.ds(middle, count + extra - middle)]
    for j in range(blocks):
        for group in groups:
            value = state[group, block(j)]
            if j:
                value = value - times_exact(
                    (y_high[group, block(j - 1)], y_low[group, block(j - 1)]),
                    lower[block(j), block(j - 1)],
                    dot_nt,
                )
            value = times_pair(split(value), (inv_high[j], inv_low[j]), dot_nt)
            state[group, block(j)] = value
            y_high[group, block(j)], y_low[group, block(j)] = split(value)
            if 1 <= j < blocks - 1:
                done = pl.ds(0, BLOCK * j)
                state[group, block(j + 1)] = state[group, block(j + 1)] - times_exact(
                    (y_high[group, done], y_low[group, done]), lower[block(j + 1), done], dot_nt
                )
    for j in reversed(range(blocks)):
        for group in groups:
            value = state[group, block(j)]
            if j < blocks - 1:
                value = value - times_exact(
                    (out_high[group, block(j + 1)], out_low[group, block(j + 1)]),
                    lower[block(j + 1), block(j)],
                    dot_nn,
                )
            value = times_pair(split(value), (inv_high[j], inv_low[j]), dot_nn)
            out_high[group, block(j)], out_low[group, block(j)] = split(value)
            if 1 <= j < blocks - 1:
                done = pl.ds(BLOCK * (j + 1), BLOCK * (blocks - 1 - j))
                state[group, block(j - 1)] = state[group, block(j - 1)] - times_exact(
                    (out_high[group, done], out_low[group, done]), lower[done, block(j - 1)], dot_nn
                )


def solve(where, factor, train, query, extra):
    count, width = train.shape
    rows = count + extra
    blocks = width // BLOCK
    pair = jax.ShapeDtypeStruct((rows, width), BF16)
    train_pair = jax.ShapeDtypeStruct((count, width), BF16)
    return pl.pallas_call(
        solve_kernel,
        out_shape=(pair, pair, train_pair, train_pair),
        in_specs=[pl.BlockSpec(memory_space=pltpu.SMEM)] + [pl.BlockSpec(memory_space=pltpu.HBM)] * 3,
        out_specs=(pl.BlockSpec(memory_space=pltpu.VMEM),) * 4,
        scratch_shapes=[
            pltpu.VMEM((width, width), BF16),
            pltpu.VMEM((rows, width), F32),
            pltpu.VMEM((rows, width), BF16),
            pltpu.VMEM((rows, width), BF16),
            pltpu.VMEM((blocks, BLOCK, BLOCK), BF16),
            pltpu.VMEM((blocks, BLOCK, BLOCK), BF16),
            pltpu.SemaphoreType.DMA((2 * blocks + 1,)),
        ],
        compiler_params=pltpu.CompilerParams(vmem_limit_bytes=48 * 1024 * 1024),
        cost_estimate=pl.CostEstimate(
            flops=12 * rows * width * width, bytes_accessed=16 * 1024 * 1024, transcendentals=0
        ),
        name="solve",
    )(where, factor, train, query)


def product_terms(where, order_at, places, pair, high, low, train_high, train_low, out):
    n_rows, count = pair[0].shape
    extra = high.shape[0] - count
    half = n_rows // 2
    order, flip = where[order_at], where[order_at + 1]
    offset = pl.multiple_of(where[2] ^ (flip * half), extra)
    factor = jnp.where(where[3] > 0, 0.5, 0.0).astype(F32)
    for at, place in enumerate(places):
        columns = pl.ds(pl.multiple_of((order ^ place) * BLOCK, BLOCK), BLOCK)
        found = times_pair(pair, (train_high[:, columns], train_low[:, columns]), dot_nn)
        for r in range(2):
            out[at, pl.ds(pl.multiple_of((r ^ flip) * half, half), half), :] = found[r * half : (r + 1) * half]
        first = high[pl.ds(count, extra), columns].astype(F32) + low[pl.ds(count, extra), columns].astype(F32)
        out[at, pl.ds(offset, extra), :] = out[at, pl.ds(offset, extra), :] + factor * first


def first_scores(pieces, high, low, rows_buf):
    piece_rows, count = pieces[0].shape[0], rows_buf.shape[0] // 2
    for r, piece in enumerate(pieces):
        part_high, part_low = split(piece[...])
        rows_buf[r * piece_rows : (r + 1) * piece_rows, :] = part_high
        rows_buf[count + r * piece_rows : count + (r + 1) * piece_rows, :] = part_low
    both = dot_nt(rows_buf[...], high)
    return both[:count] + both[count:] + dot_nt(rows_buf[0:count, :], low)


def near_kernel(where, *refs):
    high, low, out, rows_buf = refs[-4:]
    count = out.shape[1]
    out[...] = first_scores(refs[:-4], high[0:count, :], low[0:count, :], rows_buf)


def send_kernel(scale, near_places, chunk_places, where, *refs):
    pieces = refs[:-10]
    near, high, low, train_high, train_low, scores, pair_high, pair_low, send, rows_buf = refs[-10:]
    piece_rows = pieces[0].shape[0]
    count = scores.shape[1]
    far = first_scores(pieces, high[0:count, :], low[0:count, :], rows_buf)
    far_places = [r for r in range(len(pieces) + len(near_places)) if r not in near_places]
    for source, places in ((near[...], near_places), (far, far_places)):
        for i, r in enumerate(places):
            offset = pl.multiple_of((where[0] ^ r) * piece_rows, piece_rows)
            scores[pl.ds(offset, piece_rows), :] = source[i * piece_rows : (i + 1) * piece_rows]
    pair = split(scores[...] * scale)
    pair_high[...], pair_low[...] = pair
    product_terms(where, 6, chunk_places, pair, high, low, train_high, train_low, send)


def terms_kernel(order_at, places, where, pair_high, pair_low, high, low, train_high, train_low, out):
    pair = (pair_high[...], pair_low[...])
    product_terms(where, order_at, places, pair, high, low, train_high, train_low, out)


def on_vmem(kernel, out_shape, scratch, flops, name, where, *args):
    return pl.pallas_call(
        kernel,
        out_shape=out_shape,
        in_specs=[pl.BlockSpec(memory_space=pltpu.SMEM)] + [pl.BlockSpec(memory_space=pltpu.VMEM)] * len(args),
        out_specs=jax.tree.map(lambda _: pl.BlockSpec(memory_space=pltpu.VMEM), out_shape),
        scratch_shapes=scratch,
        compiler_params=pltpu.CompilerParams(vmem_limit_bytes=40 * 1024 * 1024),
        cost_estimate=pl.CostEstimate(flops=flops, bytes_accessed=4 * 1024 * 1024, transcendentals=0),
        name=name,
    )(where, *args)


def final_kernel(groups, twice, scale, where, total, *refs):
    parts = refs[:-3]
    high, low, out = refs[-3:]
    count = out.shape[1]
    half = out.shape[0] // 2
    result = total[...]
    if twice:
        result = result * 2.0
    for part, (order_at, places) in zip(parts, groups):
        order, flip = where[order_at], where[order_at + 1]
        for at, place in enumerate(places):
            columns = pl.ds(pl.multiple_of((order ^ place) * BLOCK, BLOCK), BLOCK)
            rows = jnp.concatenate(
                [part[at, pl.ds(pl.multiple_of((r ^ flip) * half, half), half), :] for r in range(2)], axis=0
            )
            result = result - times_pair(split(rows), (high[0:count, columns], low[0:count, columns]), dot_nt)
    out[...] = result * scale


def bits(size):
    assert size & (size - 1) == 0
    return [1 << i for i in range(size.bit_length() - 1)]


def shards(queries, train_grads, factor):
    n_query, n_data = lax.axis_size("query"), lax.axis_size("dp")
    query_pos, data_pos = lax.axis_index("query"), lax.axis_index("dp")
    query_rows, width = queries.shape
    total_train = train_grads.shape[0] * n_data * n_query
    ranks = range(n_query * n_data)

    def swap(value, even, odd=None):
        odd = even if odd is None else odd
        return lax.ppermute(value, AXES, [(r, r ^ (odd if r & 1 else even)) for r in ranks])

    x_bits, z_bits = bits(n_query)[1:], [n_query * b for b in bits(n_data)]
    parity = {bit: bit for bit in [1] + x_bits + z_bits}
    if len(z_bits) > 1:
        parity[z_bits[0]] = z_bits[1] = z_bits[0] | z_bits[1]
    evens, odds = [], []
    for i in range(max(len(x_bits), len(z_bits))):
        evens += z_bits[i : i + 1] + x_bits[i : i + 1]
        odds += x_bits[i : i + 1] + z_bits[i : i + 1]
    steps = [(1, 1)] + list(zip(evens, odds))
    turned = steps[:1] + [(odd, even) for even, odd in steps[1:3]] + steps[3:]
    steps_of = [steps, turned]

    extra = max(16, query_rows // n_data)
    taken = data_pos * extra < query_rows
    start = jnp.where(taken, data_pos * extra, 0)
    rank = data_pos * n_query + query_pos
    n_pieces = width // BLOCK

    def order_of(rank, steps):
        chosen = [rank & jnp.where(rank & 1, parity[odd], parity[even]) for even, odd in steps[:3]]
        chosen = [lax.population_count(bits_set) % 2 for bits_set in chosen]
        return [chosen[0] * (n_pieces // 2) + chosen[1] * (n_pieces // 4), chosen[2]]

    where = jnp.stack(
        [query_pos, start, query_pos * query_rows + start, taken.astype(jnp.int32)]
        + order_of(rank, steps)
        + order_of(rank ^ 1, steps)
        + order_of(rank, turned)
        + order_of(rank ^ 1, turned)
    )

    pieces = {0: queries}
    for bit in x_bits:
        pieces |= {r | bit: swap(piece, bit) for r, piece in pieces.items()}
    pieces[1] = swap(queries, 1)
    high, low, train_high, train_low = solve(where, factor, train_grads, queries, extra)
    near_places = [0, 1] + list(range(2, n_query, 2))
    pieces, high = lax.optimization_barrier((pieces, high))
    far = [swap(pieces[r], 1) for r in range(2, n_query, 2)]
    near = on_vmem(
        near_kernel,
        jax.ShapeDtypeStruct((len(near_places) * query_rows, train_grads.shape[0]), F32),
        [pltpu.VMEM((2 * len(near_places) * query_rows, width), BF16)],
        6 * len(near_places) * query_rows * width * train_grads.shape[0],
        "near_scores",
        where,
        *[pieces[r] for r in near_places],
        high,
        low,
    )

    n_rows, count = n_query * query_rows, train_grads.shape[0]
    quarter, half = n_pieces // 4, n_rows // 2
    lead = quarter // 2
    places_of = [[q * quarter + c * lead + p for q in range(2) for p in range(lead)] for c in range(2)]
    scores_shape = jax.ShapeDtypeStruct((n_rows, count), F32)
    pair_shape = jax.ShapeDtypeStruct((n_rows, count), BF16)
    chunk_shape = jax.ShapeDtypeStruct((quarter, n_rows, BLOCK), F32)
    operands = (high, low, train_high, train_low)
    flops = 3 * n_rows * width * count
    scores, pair_high, pair_low, send = on_vmem(
        functools.partial(send_kernel, 1.0 / total_train, near_places, places_of[0]),
        (scores_shape, pair_shape, pair_shape, chunk_shape),
        [pltpu.VMEM((2 * len(far) * query_rows, width), BF16)],
        flops,
        "scores_and_send",
        where,
        *far,
        near,
        *operands,
    )

    def terms(order_at, places, name, high_part):
        kernel = functools.partial(terms_kernel, order_at, places)
        return on_vmem(kernel, chunk_shape, [], flops // 2, name, where, high_part, pair_low, *operands)

    got_first = swap(send, *steps[0])
    got_second = swap(terms(10, places_of[1], "send_second", pair_high), *steps[0])
    got = [got_first, got_second]
    keep = [terms(4, places_of[0], "keep_first", pair_high)]

    chunks = []
    for c in range(2):
        places = places_of[c]
        mine = keep[c][:lead] + got[c][:lead]
        theirs = keep[c][lead:] + got[c][lead:]
        if c == 0:
            theirs, later = lax.optimization_barrier((theirs, pair_high))
            keep.append(terms(8, places_of[1], "keep_second", later))
        moved = swap(theirs, *steps_of[c][1])
        mine, theirs = mine[:, :half] + moved[:, :half], mine[:, half:] + moved[:, half:]
        mine = mine + swap(theirs, *steps_of[c][2])
        for step in steps_of[c][3:]:
            mine = mine + swap(mine, *step)
        mine = jnp.concatenate([mine, swap(mine, *steps_of[c][2])], axis=1)
        mine = jnp.concatenate([mine, swap(mine, *steps_of[c][1])], axis=0)
        chunks.append((mine, places))

    def subtract(total, parts, groups, twice, scale, name):
        kernel = functools.partial(final_kernel, groups, twice, scale)
        count = sum(len(places) for _, places in groups)
        return on_vmem(
            kernel, scores_shape, [], 2 * flops * count // n_pieces, name, where, total, *parts, high, low
        )

    (own_a, places_a), (own_b, places_b) = chunks
    total = subtract(scores, [own_a], [(4, places_a)], True, 1.0, "own_first")
    own_a, total = lax.optimization_barrier((own_a, total))
    other_a = swap(own_a, *steps[0])
    other_b = swap(own_b, *steps[0])
    total = subtract(total, [own_b, other_a], [(8, places_b), (6, places_a)], False, 1.0, "own_second")
    return subtract(total, [other_b], [(10, places_b)], False, width**-0.5, "other_second")


def solution(mesh):
    in_specs = (P(("groups", "query"), None), P(("groups", "dp", "query"), None), P("groups", None))
    out_specs = P("groups", ("dp", "query"))
    return jax.shard_map(shards, mesh=mesh, in_specs=in_specs, out_specs=out_specs, check_vma=False)
```

```python
import functools

import jax
import jax.numpy as jnp
from jax import lax
from jax.experimental import pallas as pl
from jax.experimental.pallas import tpu as pltpu
from jax.sharding import PartitionSpec as P

BLOCK = 256
HALF = 128
BASE = 16
AXES = ("dp", "query")
F32 = jnp.float32
BF16 = jnp.bfloat16


def split(value):
    high = value.astype(BF16)
    return high, (value - high.astype(F32)).astype(BF16)


def dot_nn(left, right):
    return lax.dot_general(left, right, (((1,), (0,)), ((), ())), preferred_element_type=F32)


def dot_nt(left, right):
    return lax.dot_general(left, right, (((1,), (1,)), ((), ())), preferred_element_type=F32)


def times_exact(left_pair, right, dot):
    rows = left_pair[0].shape[0]
    both = dot(jnp.concatenate(left_pair, axis=0), right)
    return both[:rows] + both[rows:]


def times_pair(left_pair, right_pair, dot):
    return times_exact(left_pair, right_pair[0], dot) + dot(left_pair[0], right_pair[1])


def invert_diagonals(lower, inv_high, inv_low, blocks):
    count = blocks * (BLOCK // HALF)
    row = lax.broadcasted_iota(jnp.int32, (HALF, HALF), 0)
    lane = lax.broadcasted_iota(jnp.int32, (HALF, HALF), 1)
    same = (row // BASE) == (lane // BASE)
    diagonals = [lower[pl.ds(HALF * g, HALF), pl.ds(HALF * g, HALF)].astype(F32) for g in range(count)]
    packed = []
    for diagonal in diagonals:
        kept = jnp.where(same, diagonal, 0.0)
        total = kept[0:BASE]
        for s in range(1, HALF // BASE):
            total = total + kept[s * BASE : (s + 1) * BASE]
        packed.append(total)
    packed = jnp.concatenate(packed, axis=0).astype(BF16)
    shape = (count, BASE, HALF)
    in_row = lax.broadcasted_iota(jnp.int32, shape, 1)
    in_lane = lax.broadcasted_iota(jnp.int32, shape, 2) % BASE
    solved = jnp.where(in_row == in_lane, 1.0, 0.0).astype(F32)
    for k in range(BASE):
        spread = jnp.where(row == (lane // BASE) * BASE + k, 1.0, 0.0).astype(BF16)
        column = dot_nn(packed, spread).reshape(shape)
        pivot_row = solved[:, k : k + 1, :] / column[:, k : k + 1, :]
        below = solved - column * pivot_row
        solved = jnp.where(in_row == k, pivot_row, jnp.where(in_row > k, below, solved))
    inverses = []
    for g in range(count):
        tiled = jnp.concatenate([solved[g]] * (HALF // BASE), axis=0)
        inverses.append(jnp.where(same, tiled, 0.0))
    size = BASE
    while size < HALF:
        part = (row // (2 * size) == lane // (2 * size)) & ((row // size) % 2 == 1) & ((lane // size) % 2 == 0)
        pairs = [split(x) for x in inverses]
        middles = []
        for g in range(count):
            below = jnp.where(part, diagonals[g], 0.0).astype(BF16)
            middles.append(
                dot_nn(jnp.concatenate([below, below], axis=1), jnp.concatenate(pairs[g], axis=0))
            )
        for g in range(count):
            mid_high, mid_low = split(middles[g])
            change = dot_nn(
                jnp.concatenate(pairs[g], axis=1), jnp.concatenate([mid_high, mid_high], axis=0)
            ) + dot_nn(pairs[g][0], mid_low)
            inverses[g] = inverses[g] - change
        size *= 2
    for j in range(blocks):
        upper, under = split(inverses[2 * j]), split(inverses[2 * j + 1])
        below = lower[pl.ds(BLOCK * j + HALF, HALF), pl.ds(BLOCK * j, HALF)]
        middle = dot_nn(jnp.concatenate([below, below], axis=1), jnp.concatenate(upper, axis=0))
        mid_high, mid_low = split(middle)
        corner = dot_nn(
            jnp.concatenate(under, axis=1), jnp.concatenate([mid_high, mid_high], axis=0)
        ) + dot_nn(under[0], mid_low)
        corner = split(-corner)
        zero = jnp.zeros((HALF, HALF), BF16)
        for part, out in ((0, inv_high), (1, inv_low)):
            out[j, 0:HALF, 0:HALF] = upper[part]
            out[j, 0:HALF, HALF:BLOCK] = zero
            out[j, HALF:BLOCK, 0:HALF] = corner[part]
            out[j, HALF:BLOCK, HALF:BLOCK] = under[part]


def solve_kernel(
    where, factor, train, query, out_high, out_low, train_high, train_low,
    lower, state, y_high, y_low, inv_high, inv_low, sems,
):
    blocks = factor.shape[0] // BLOCK
    count = train.shape[0]
    extra = state.shape[0] - count

    def block(j):
        return pl.ds(BLOCK * j, BLOCK)

    def fetch(source, target, at):
        return pltpu.make_async_copy(source, target, sems.at[at])

    diagonal = [
        fetch(factor.at[block(j), block(j)], lower.at[block(j), block(j)], j) for j in range(blocks)
    ]
    start = pl.multiple_of(where[1], extra)
    rest = [
        fetch(train, state.at[pl.ds(0, count), :], blocks),
        fetch(query.at[pl.ds(start, extra), :], state.at[pl.ds(count, extra), :], blocks + 1),
    ]
    for j in range(1, blocks):
        columns = pl.ds(0, BLOCK * j)
        rest.append(fetch(factor.at[block(j), columns], lower.at[block(j), columns], blocks + 1 + j))
    for copy in diagonal + rest:
        copy.start()
    for copy in diagonal:
        copy.wait()
    invert_diagonals(lower, inv_high, inv_low, blocks)
    for copy in rest:
        copy.wait()
    train_high[...], train_low[...] = split(state[0:count, :])

    middle = 16 * -(-(count + extra) // 32)
    groups = [pl.ds(0, middle), pl.ds(middle, count + extra - middle)]
    for j in range(blocks):
        for group in groups:
            value = state[group, block(j)]
            if j:
                value = value - times_exact(
                    (y_high[group, block(j - 1)], y_low[group, block(j - 1)]),
                    lower[block(j), block(j - 1)],
                    dot_nt,
                )
            value = times_pair(split(value), (inv_high[j], inv_low[j]), dot_nt)
            state[group, block(j)] = value
            y_high[group, block(j)], y_low[group, block(j)] = split(value)
            if 1 <= j < blocks - 1:
                done = pl.ds(0, BLOCK * j)
                state[group, block(j + 1)] = state[group, block(j + 1)] - times_exact(
                    (y_high[group, done], y_low[group, done]), lower[block(j + 1), done], dot_nt
                )
    for j in reversed(range(blocks)):
        for group in groups:
            value = state[group, block(j)]
            if j < blocks - 1:
                value = value - times_exact(
                    (out_high[group, block(j + 1)], out_low[group, block(j + 1)]),
                    lower[block(j + 1), block(j)],
                    dot_nn,
                )
            value = times_pair(split(value), (inv_high[j], inv_low[j]), dot_nn)
            out_high[group, block(j)], out_low[group, block(j)] = split(value)
            if 1 <= j < blocks - 1:
                done = pl.ds(BLOCK * (j + 1), BLOCK * (blocks - 1 - j))
                state[group, block(j - 1)] = state[group, block(j - 1)] - times_exact(
                    (out_high[group, done], out_low[group, done]), lower[done, block(j - 1)], dot_nn
                )


def solve(where, factor, train, query, extra):
    count, width = train.shape
    rows = count + extra
    blocks = width // BLOCK
    pair = jax.ShapeDtypeStruct((rows, width), BF16)
    train_pair = jax.ShapeDtypeStruct((count, width), BF16)
    return pl.pallas_call(
        solve_kernel,
        out_shape=(pair, pair, train_pair, train_pair),
        in_specs=[pl.BlockSpec(memory_space=pltpu.SMEM)] + [pl.BlockSpec(memory_space=pltpu.HBM)] * 3,
        out_specs=(pl.BlockSpec(memory_space=pltpu.VMEM),) * 4,
        scratch_shapes=[
            pltpu.VMEM((width, width), BF16),
            pltpu.VMEM((rows, width), F32),
            pltpu.VMEM((rows, width), BF16),
            pltpu.VMEM((rows, width), BF16),
            pltpu.VMEM((blocks, BLOCK, BLOCK), BF16),
            pltpu.VMEM((blocks, BLOCK, BLOCK), BF16),
            pltpu.SemaphoreType.DMA((2 * blocks + 1,)),
        ],
        compiler_params=pltpu.CompilerParams(vmem_limit_bytes=48 * 1024 * 1024),
        cost_estimate=pl.CostEstimate(
            flops=12 * rows * width * width, bytes_accessed=16 * 1024 * 1024, transcendentals=0
        ),
        name="solve",
    )(where, factor, train, query)


def product_terms(where, order_at, places, pair, high, low, train_high, train_low, out):
    n_rows, count = pair[0].shape
    extra = high.shape[0] - count
    half = n_rows // 2
    order, flip = where[order_at], where[order_at + 1]
    offset = pl.multiple_of(where[2] ^ (flip * half), extra)
    factor = jnp.where(where[3] > 0, 0.5, 0.0).astype(F32)
    for at, place in enumerate(places):
        columns = pl.ds(pl.multiple_of((order ^ place) * BLOCK, BLOCK), BLOCK)
        found = times_pair(pair, (train_high[:, columns], train_low[:, columns]), dot_nn)
        for r in range(2):
            out[at, pl.ds(pl.multiple_of((r ^ flip) * half, half), half), :] = found[r * half : (r + 1) * half]
        first = high[pl.ds(count, extra), columns].astype(F32) + low[pl.ds(count, extra), columns].astype(F32)
        out[at, pl.ds(offset, extra), :] = out[at, pl.ds(offset, extra), :] + factor * first


def first_scores(pieces, high, low, rows_buf):
    piece_rows, count = pieces[0].shape[0], rows_buf.shape[0] // 2
    for r, piece in enumerate(pieces):
        part_high, part_low = split(piece[...])
        rows_buf[r * piece_rows : (r + 1) * piece_rows, :] = part_high
        rows_buf[count + r * piece_rows : count + (r + 1) * piece_rows, :] = part_low
    both = dot_nt(rows_buf[...], high)
    return both[:count] + both[count:] + dot_nt(rows_buf[0:count, :], low)


def near_kernel(where, *refs):
    high, low, out, rows_buf = refs[-4:]
    count = out.shape[1]
    out[...] = first_scores(refs[:-4], high[0:count, :], low[0:count, :], rows_buf)


def send_kernel(scale, near_places, chunk_places, where, *refs):
    pieces = refs[:-10]
    near, high, low, train_high, train_low, scores, pair_high, pair_low, send, rows_buf = refs[-10:]
    piece_rows = pieces[0].shape[0]
    count = scores.shape[1]
    far = first_scores(pieces, high[0:count, :], low[0:count, :], rows_buf)
    far_places = [r for r in range(len(pieces) + len(near_places)) if r not in near_places]
    for source, places in ((near[...], near_places), (far, far_places)):
        for i, r in enumerate(places):
            offset = pl.multiple_of((where[0] ^ r) * piece_rows, piece_rows)
            scores[pl.ds(offset, piece_rows), :] = source[i * piece_rows : (i + 1) * piece_rows]
    pair = split(scores[...] * scale)
    pair_high[...], pair_low[...] = pair
    product_terms(where, 6, chunk_places, pair, high, low, train_high, train_low, send)


def terms_kernel(order_at, places, where, pair_high, pair_low, high, low, train_high, train_low, out):
    pair = (pair_high[...], pair_low[...])
    product_terms(where, order_at, places, pair, high, low, train_high, train_low, out)


def on_vmem(kernel, out_shape, scratch, flops, name, where, *args):
    return pl.pallas_call(
        kernel,
        out_shape=out_shape,
        in_specs=[pl.BlockSpec(memory_space=pltpu.SMEM)] + [pl.BlockSpec(memory_space=pltpu.VMEM)] * len(args),
        out_specs=jax.tree.map(lambda _: pl.BlockSpec(memory_space=pltpu.VMEM), out_shape),
        scratch_shapes=scratch,
        compiler_params=pltpu.CompilerParams(vmem_limit_bytes=40 * 1024 * 1024),
        cost_estimate=pl.CostEstimate(flops=flops, bytes_accessed=4 * 1024 * 1024, transcendentals=0),
        name=name,
    )(where, *args)


def final_kernel(groups, twice, scale, where, total, *refs):
    parts = refs[:-3]
    high, low, out = refs[-3:]
    count = out.shape[1]
    half = out.shape[0] // 2
    result = total[...]
    if twice:
        result = result * 2.0
    for part, (order_at, places) in zip(parts, groups):
        order, flip = where[order_at], where[order_at + 1]
        for at, place in enumerate(places):
            columns = pl.ds(pl.multiple_of((order ^ place) * BLOCK, BLOCK), BLOCK)
            rows = jnp.concatenate(
                [part[at, pl.ds(pl.multiple_of((r ^ flip) * half, half), half), :] for r in range(2)], axis=0
            )
            result = result - times_pair(split(rows), (high[0:count, columns], low[0:count, columns]), dot_nt)
    out[...] = result * scale


def bits(size):
    assert size & (size - 1) == 0
    return [1 << i for i in range(size.bit_length() - 1)]


def shards(queries, train_grads, factor):
    n_query, n_data = lax.axis_size("query"), lax.axis_size("dp")
    query_pos, data_pos = lax.axis_index("query"), lax.axis_index("dp")
    query_rows, width = queries.shape
    total_train = train_grads.shape[0] * n_data * n_query
    ranks = range(n_query * n_data)

    def swap(value, even, odd=None):
        odd = even if odd is None else odd
        return lax.ppermute(value, AXES, [(r, r ^ (odd if r & 1 else even)) for r in ranks])

    x_bits, z_bits = bits(n_query)[1:], [n_query * b for b in bits(n_data)]
    parity = {bit: bit for bit in [1] + x_bits + z_bits}
    if len(z_bits) > 1:
        parity[z_bits[0]] = z_bits[1] = z_bits[0] | z_bits[1]
    evens, odds = [], []
    for i in range(max(len(x_bits), len(z_bits))):
        evens += z_bits[i : i + 1] + x_bits[i : i + 1]
        odds += x_bits[i : i + 1] + z_bits[i : i + 1]
    steps = [(1, 1)] + list(zip(evens, odds))
    turned = steps[:1] + [(odd, even) for even, odd in steps[1:3]] + steps[3:]
    steps_of = [steps, turned]

    extra = max(16, query_rows // n_data)
    taken = data_pos * extra < query_rows
    start = jnp.where(taken, data_pos * extra, 0)
    rank = data_pos * n_query + query_pos
    n_pieces = width // BLOCK

    def order_of(rank, steps):
        chosen = [rank & jnp.where(rank & 1, parity[odd], parity[even]) for even, odd in steps[:3]]
        chosen = [lax.population_count(bits_set) % 2 for bits_set in chosen]
        return [chosen[0] * (n_pieces // 2) + chosen[1] * (n_pieces // 4), chosen[2]]

    where = jnp.stack(
        [query_pos, start, query_pos * query_rows + start, taken.astype(jnp.int32)]
        + order_of(rank, steps)
        + order_of(rank ^ 1, steps)
        + order_of(rank, turned)
        + order_of(rank ^ 1, turned)
    )

    pieces = {0: queries}
    for bit in x_bits:
        pieces |= {r | bit: swap(piece, bit) for r, piece in pieces.items()}
    pieces[1] = swap(queries, 1)
    high, low, train_high, train_low = solve(where, factor, train_grads, queries, extra)
    near_places = [0, 1] + list(range(2, n_query, 2))
    pieces, high = lax.optimization_barrier((pieces, high))
    far = [swap(pieces[r], 1) for r in range(2, n_query, 2)]
    near = on_vmem(
        near_kernel,
        jax.ShapeDtypeStruct((len(near_places) * query_rows, train_grads.shape[0]), F32),
        [pltpu.VMEM((2 * len(near_places) * query_rows, width), BF16)],
        6 * len(near_places) * query_rows * width * train_grads.shape[0],
        "near_scores",
        where,
        *[pieces[r] for r in near_places],
        high,
        low,
    )

    n_rows, count = n_query * query_rows, train_grads.shape[0]
    quarter, half = n_pieces // 4, n_rows // 2
    lead = quarter // 2
    places_of = [[q * quarter + c * lead + p for q in range(2) for p in range(lead)] for c in range(2)]
    scores_shape = jax.ShapeDtypeStruct((n_rows, count), F32)
    pair_shape = jax.ShapeDtypeStruct((n_rows, count), BF16)
    chunk_shape = jax.ShapeDtypeStruct((quarter, n_rows, BLOCK), F32)
    operands = (high, low, train_high, train_low)
    flops = 3 * n_rows * width * count
    scores, pair_high, pair_low, send = on_vmem(
        functools.partial(send_kernel, 1.0 / total_train, near_places, places_of[0]),
        (scores_shape, pair_shape, pair_shape, chunk_shape),
        [pltpu.VMEM((2 * len(far) * query_rows, width), BF16)],
        flops,
        "scores_and_send",
        where,
        *far,
        near,
        *operands,
    )

    def terms(order_at, places, name, high_part):
        kernel = functools.partial(terms_kernel, order_at, places)
        return on_vmem(kernel, chunk_shape, [], flops // 2, name, where, high_part, pair_low, *operands)

    got_first = swap(send, *steps[0])
    got_second = swap(terms(10, places_of[1], "send_second", pair_high), *steps[0])
    got = [got_first, got_second]
    keep = [terms(4, places_of[0], "keep_first", pair_high)]

    chunks = []
    for c in range(2):
        places = places_of[c]
        mine = keep[c][:lead] + got[c][:lead]
        theirs = keep[c][lead:] + got[c][lead:]
        if c == 0:
            theirs, later = lax.optimization_barrier((theirs, pair_high))
            keep.append(terms(8, places_of[1], "keep_second", later))
        if c == 1:
            theirs, _ = lax.optimization_barrier((theirs, moved))
        moved = swap(theirs, *steps_of[c][1])
        mine, theirs = mine[:, :half] + moved[:, :half], mine[:, half:] + moved[:, half:]
        mine = mine + swap(theirs, *steps_of[c][2])
        for step in steps_of[c][3:]:
            mine = mine + swap(mine, *step)
        mine = jnp.concatenate([mine, swap(mine, *steps_of[c][2])], axis=1)
        mine = jnp.concatenate([mine, swap(mine, *steps_of[c][1])], axis=0)
        chunks.append((mine, places))

    def subtract(total, parts, groups, twice, scale, name):
        kernel = functools.partial(final_kernel, groups, twice, scale)
        count = sum(len(places) for _, places in groups)
        return on_vmem(
            kernel, scores_shape, [], 2 * flops * count // n_pieces, name, where, total, *parts, high, low
        )

    (own_a, places_a), (own_b, places_b) = chunks
    total = subtract(scores, [own_a], [(4, places_a)], True, 1.0, "own_first")
    own_a, total = lax.optimization_barrier((own_a, total))
    other_a = swap(own_a, *steps[0])
    other_b = swap(own_b, *steps[0])
    total = subtract(total, [own_b, other_a], [(8, places_b), (6, places_a)], False, 1.0, "own_second")
    return subtract(total, [other_b], [(10, places_b)], False, width**-0.5, "other_second")


def solution(mesh):
    in_specs = (P(("groups", "query"), None), P(("groups", "dp", "query"), None), P("groups", None))
    out_specs = P("groups", ("dp", "query"))
    return jax.shard_map(shards, mesh=mesh, in_specs=in_specs, out_specs=out_specs, check_vma=False)
```
